128 devices in a mesh: samp: 16 (over z_hi, y, core), feat: 8 (over z_lo, x).
Axes of the slice: x: 4, y: 4, z: 4 (z_hi: 2, z_lo: 2; z = z_hi * 2 + z_lo), core: 2. Of those that a mesh axis runs over, the one named last changes fastest.
Arguments:
- noise: bfloat16 [4096, 32768], P('samp', 'feat'), may hold values from -24 to 24
- data: bfloat16 [4096, 32768], P('samp', 'feat'), may hold values from -6 to 6
Outputs:
- targets: bfloat16 [4096, 32768], P('samp', 'feat')
- column_potential: float32 [4096], P('feat')
The draws below stay inside these ranges and needn't reach their ends.
All inputs are finite; a program needn't handle non-finite values.
Results may differ from the reference program's by a relative error of at most 0.0065.
Values may be sent and summed in bfloat16 or wider, within the bound.
No kernel may reach another device: no remote copies, remote signals or barrier semaphores. Data moves between devices by JAX's collectives and lax.ppermute only.
A program may use at most 128 MiB of HBM per device.

```python
import math
import jax
import jax.numpy as jnp
from jax import lax

F = 32768
ITERS = 3
SAMPLES = 4096


def draw_noise(key, part):
    key = jax.random.fold_in(key, 11)
    base_key, scale_key = jax.random.split(key)
    base = jnp.clip(jax.random.normal(base_key, (SAMPLES, F), jnp.float32), -6.0, 6.0)
    row_scale = jnp.exp(jax.random.uniform(scale_key, (SAMPLES, 1), jnp.float32, 0.0, math.log(4.0)))
    return (base * row_scale).astype(jnp.bfloat16)


def levels(key, dims, pieces, least, high):
    factor_of = 1.0
    for position, parts in pieces:
        steps = jax.random.uniform(jax.random.fold_in(jax.random.fold_in(key, 6), position), (parts,), jnp.float32, least / len(pieces), high / len(pieces))
        factor_of = factor_of * jnp.repeat(jnp.exp(steps), dims[position] // parts).reshape((-1,) + (1,) * (len(dims) - 1 - position))
    return factor_of


def bell_draw(stream_key, extent, spread, reach, pieces=(), dtype=jnp.bfloat16):
    loudness = levels(stream_key, extent, pieces, -0.22, 0.18) if pieces else 1.0
    entries = jax.random.normal(stream_key, extent, jnp.float32) * spread * loudness
    return jnp.minimum(jnp.maximum(entries, -reach), reach).astype(dtype)


def setup_inputs(seed: int = 0) -> dict:
    splits = jax.random.split(jax.random.key(seed), 3)
    noise = draw_noise(jax.random.fold_in(splits[2], 71), 0)
    data = bell_draw(splits[1], (SAMPLES, F), 1.0, 6.0, ((0, 16), (1, 8)))
    return {"noise": noise, "data": data}


def build_cost(noise, data):
    data_square = lax.optimization_barrier(jnp.sum(jnp.square(data.astype(jnp.float32)), axis=1))
    stride_rows = math.gcd(256, SAMPLES)
    blocks = noise.reshape(SAMPLES // stride_rows, stride_rows, F)

    def one_block(block):
        inner = lax.dot_general(block, data, (((1,), (1,)), ((), ())), preferred_element_type=jnp.float32)
        block_square = lax.optimization_barrier(jnp.sum(jnp.square(block.astype(jnp.float32)), axis=1))
        return (block_square[:, None] + data_square[None, :] - 2.0 * inner) / F
    return lax.map(one_block, blocks).reshape(SAMPLES, SAMPLES)

def reference(noise, data):
    cost = build_cost(noise, data)
    temper = 0.5 / math.sqrt(F)
    column_potential = jnp.zeros((SAMPLES,), jnp.float32)
    for step in range(ITERS):
        row_potential = -temper * jax.scipy.special.logsumexp((column_potential[None, :] - cost) / temper, axis=1)
        column_potential = -temper * jax.scipy.special.logsumexp((row_potential[:, None] - cost) / temper, axis=0)
    weights = jax.nn.softmax((column_potential[None, :] - cost) / temper, axis=1).astype(jnp.bfloat16)
    targets = jnp.dot(weights, data, preferred_element_type=jnp.float32).astype(jnp.bfloat16)
    return (targets, column_potential)
```

```python
import functools
import math

import jax
import jax.numpy as jnp
from jax import lax
from jax.experimental import pallas as pl
from jax.experimental.pallas import tpu as pltpu
from jax.sharding import PartitionSpec as P

F = 32768
ITERS = 3
SAMPLES = 4096
LANES = 128
ROWS = 32
GROUP = 4


def tile_list(shapes):
    return [
        (k, g, n)
        for k, (_, groups, _, width) in enumerate(shapes)
        for g in range(groups)
        for n in range(0, width, LANES)
    ]


def row_pass(tiles, blocks, logits, c_ref, peak_ref, row_ref):
    def tile(f, t):
        k, g, n = tiles[t]
        return logits[k][f, g, :, n:n + LANES] + c_ref[:, t * LANES:(t + 1) * LANES]

    def maxima(f, _):
        acc = tile(f, 0)
        for t in range(1, len(tiles)):
            acc = jnp.maximum(acc, tile(f, t))
        peak_ref[pl.ds(f * ROWS, ROWS), :] = acc
        return 0

    lax.fori_loop(0, blocks, maxima, 0)
    peak = jnp.max(peak_ref[...], axis=1, keepdims=True)
    peak_ref[...] = jnp.broadcast_to(peak, peak_ref.shape)

    def totals(f, _):
        top = peak_ref[pl.ds(f * ROWS, ROWS), :]
        acc = jnp.exp(tile(f, 0) - top)
        for t in range(1, len(tiles)):
            acc = acc + jnp.exp(tile(f, t) - top)
        row_ref[pl.ds(f * ROWS, ROWS), :] = acc
        return 0

    lax.fori_loop(0, blocks, totals, 0)
    return jnp.sum(row_ref[...], axis=1, keepdims=True)


def sinkhorn_kernel(shapes, *refs):
    logits, (c_ref, out_ref, peak_ref, row_ref) = refs[:len(shapes)], refs[len(shapes):]
    tiles = tile_list(shapes)
    blocks = shapes[0][0]
    total = row_pass(tiles, blocks, logits, c_ref, peak_ref, row_ref)
    row_ref[...] = jnp.broadcast_to(-(peak_ref[:, 0:1] + jnp.log(total)), row_ref.shape)
    for first in range(0, len(tiles), GROUP):
        group = range(first, first + GROUP)

        def values(f, r, t):
            k, g, n = tiles[t]
            rows = row_ref[pl.ds(f * ROWS + r * 8, 8), :]
            return logits[k][f, g, r * 8:(r + 1) * 8, n:n + LANES] + rows

        def maxima(f, acc):
            for r in range(ROWS // 8):
                acc = [jnp.maximum(a, values(f, r, t)) for a, t in zip(acc, group)]
            return acc

        start = [jnp.full((8, LANES), -jnp.inf, jnp.float32) for _ in group]
        acc = lax.fori_loop(0, blocks, maxima, start)
        peaks = [jnp.max(a, axis=0, keepdims=True) for a in acc]

        def totals(f, acc):
            for r in range(ROWS // 8):
                acc = [a + jnp.exp(values(f, r, t) - p) for a, p, t in zip(acc, peaks, group)]
            return acc

        start = [jnp.zeros((8, LANES), jnp.float32) for _ in group]
        acc = lax.fori_loop(0, blocks, totals, start)
        for a, p, t in zip(acc, peaks, group):
            out_ref[0:1, t * LANES:(t + 1) * LANES] = p
            out_ref[1:2, t * LANES:(t + 1) * LANES] = jnp.sum(a, axis=0, keepdims=True)


def weights_kernel(shapes, *refs):
    logits, (c_ref, out_ref, peak_ref, row_ref) = refs[:len(shapes)], refs[len(shapes):]
    tiles = tile_list(shapes)
    blocks = shapes[0][0]
    total = row_pass(tiles, blocks, logits, c_ref, peak_ref, row_ref)
    row_ref[...] = jnp.broadcast_to(total, row_ref.shape)

    def write(f, _):
        rows = pl.ds(f * ROWS, ROWS)
        top, scale = peak_ref[rows, :], 1.0 / row_ref[rows, :]
        for t, (k, g, n) in enumerate(tiles):
            lanes = slice(t * LANES, (t + 1) * LANES)
            x = logits[k][f, g, :, n:n + LANES] + c_ref[:, lanes]
            out_ref[rows, lanes] = (jnp.exp(x - top) * scale).astype(jnp.bfloat16)
        return 0

    lax.fori_loop(0, blocks, write, 0)


def row_call(kernel, out_shape, logits, c):
    shapes = tuple(a.shape for a in logits)
    rows = shapes[0][0] * ROWS
    vmem = pl.BlockSpec(memory_space=pltpu.VMEM)
    return pl.pallas_call(
        functools.partial(kernel, shapes),
        out_shape=out_shape,
        in_specs=[vmem] * (len(logits) + 1),
        out_specs=vmem,
        scratch_shapes=[pltpu.VMEM((rows, LANES), jnp.float32)] * 2,
        compiler_params=pltpu.CompilerParams(vmem_limit_bytes=32 * 2**20),
    )(*logits, c)


def combine(a, b):
    peak = jnp.maximum(a[0], b[0])
    total = a[1] * jnp.exp(a[0] - peak) + b[1] * jnp.exp(b[0] - peak)
    return jnp.stack([peak, total])


def column_update(stats, n):
    step = 1
    while step < n:
        pairs = [(i, i ^ step) for i in range(n)]
        stats = combine(stats, lax.ppermute(stats, "samp", pairs))
        step *= 2
    return -(stats[0] + jnp.log(stats[1]))[None, :]


def local(noise, data):
    temper = 0.5 / math.sqrt(F)
    everything = lax.all_gather(data, "samp", axis=0, tiled=True)
    inner = lax.dot_general(
        noise, everything, (((1,), (1,)), ((), ())), preferred_element_type=jnp.float32
    )
    noise_square = jnp.sum(jnp.square(noise.astype(jnp.float32)), axis=1)
    data_square = jnp.sum(jnp.square(everything.astype(jnp.float32)), axis=1)
    partial = (noise_square[:, None] + data_square[None, :] - 2.0 * inner) * (-1.0 / (F * temper))
    logits = lax.psum(partial, "feat")
    rows = noise.shape[0]
    logits = [logits.reshape(rows // ROWS, 1, ROWS, SAMPLES)]
    c = jnp.zeros((1, SAMPLES), jnp.float32)
    for _ in range(ITERS):
        stats = row_call(sinkhorn_kernel, jax.ShapeDtypeStruct((2, SAMPLES), jnp.float32), logits, c)
        c = column_update(stats, lax.axis_size("samp"))
    weights = row_call(weights_kernel, jax.ShapeDtypeStruct((rows, SAMPLES), jnp.bfloat16), logits, c)
    share = SAMPLES // lax.axis_size("feat")
    start = lax.axis_index("feat") * share
    column_out = lax.dynamic_slice_in_dim(c[0] * temper, start, share, 0)
    targets = jnp.dot(weights, everything, preferred_element_type=jnp.float32).astype(jnp.bfloat16)
    return (targets, column_out)


def solution(mesh):
    in_specs = (P("samp", "feat"), P("samp", "feat"))
    out_specs = (P("samp", "feat"), P("feat"))
    return jax.shard_map(local, mesh=mesh, in_specs=in_specs, out_specs=out_specs, check_vma=False)
```

```python
import functools
import math

import jax
import jax.numpy as jnp
from jax import lax
from jax.experimental import pallas as pl
from jax.experimental.pallas import tpu as pltpu
from jax.sharding import Mesh, PartitionSpec as P

F = 32768
ITERS = 3
SAMPLES = 4096
LANES = 128
ROWS = 32
GROUP = 4
DEPTH = 1024
FEAT = ("zl", "x")


def tile_list(shapes):
    return [
        (k, g, n)
        for k, (_, groups, _, width) in enumerate(shapes)
        for g in range(groups)
        for n in range(0, width, LANES)
    ]


def row_pass(tiles, blocks, logits, where, c_ref, peak_ref, row_ref):
    def tile(f, t):
        k, g, n = tiles[t]
        return logits[k][f, g, :, n:n + LANES] + c_ref[:, lanes(where[0, t])]

    def maxima(f, _):
        acc = tile(f, 0)
        for t in range(1, len(tiles)):
            acc = jnp.maximum(acc, tile(f, t))
        peak_ref[pl.ds(f * ROWS, ROWS), :] = acc
        return 0

    lax.fori_loop(0, blocks, maxima, 0)
    peak = jnp.max(peak_ref[...], axis=1, keepdims=True)
    peak_ref[...] = jnp.broadcast_to(peak, peak_ref.shape)

    def totals(f, _):
        top = peak_ref[pl.ds(f * ROWS, ROWS), :]
        acc = jnp.exp(tile(f, 0) - top)
        for t in range(1, len(tiles)):
            acc = acc + jnp.exp(tile(f, t) - top)
        row_ref[pl.ds(f * ROWS, ROWS), :] = acc
        return 0

    lax.fori_loop(0, blocks, totals, 0)
    return jnp.sum(row_ref[...], axis=1, keepdims=True)


def lanes(tile):
    return pl.ds(pl.multiple_of(tile * LANES, LANES), LANES)


def sinkhorn_kernel(shapes, where, *refs):
    logits, (c_ref, out_ref, peak_ref, row_ref) = refs[:len(shapes)], refs[len(shapes):]
    tiles = tile_list(shapes)
    blocks = shapes[0][0]
    total = row_pass(tiles, blocks, logits, where, c_ref, peak_ref, row_ref)
    row_ref[...] = jnp.broadcast_to(-(peak_ref[:, 0:1] + jnp.log(total)), row_ref.shape)
    for first in range(0, len(tiles), GROUP):
        group = range(first, first + GROUP)

        def values(f, r, t):
            k, g, n = tiles[t]
            rows = row_ref[pl.ds(f * ROWS + r * 8, 8), :]
            return logits[k][f, g, r * 8:(r + 1) * 8, n:n + LANES] + rows

        def maxima(f, acc):
            for r in range(ROWS // 8):
                acc = [jnp.maximum(a, values(f, r, t)) for a, t in zip(acc, group)]
            return acc

        start = [jnp.full((8, LANES), -jnp.inf, jnp.float32) for _ in group]
        acc = lax.fori_loop(0, blocks, maxima, start)
        peaks = [jnp.max(a, axis=0, keepdims=True) for a in acc]

        def totals(f, acc):
            for r in range(ROWS // 8):
                acc = [a + jnp.exp(values(f, r, t) - p) for a, p, t in zip(acc, peaks, group)]
            return acc

        start = [jnp.zeros((8, LANES), jnp.float32) for _ in group]
        acc = lax.fori_loop(0, blocks, totals, start)
        for a, p, t in zip(acc, peaks, group):
            out_ref[0:1, lanes(where[0, t])] = p
            out_ref[1:2, lanes(where[0, t])] = jnp.sum(a, axis=0, keepdims=True)


def weights_kernel(shapes, where, *refs):
    logits, (c_ref, out_ref, peak_ref, row_ref) = refs[:len(shapes)], refs[len(shapes):]
    tiles = tile_list(shapes)
    blocks = shapes[0][0]
    total = row_pass(tiles, blocks, logits, where, c_ref, peak_ref, row_ref)
    row_ref[...] = jnp.broadcast_to(total, row_ref.shape)

    def write(f, _):
        rows = pl.ds(f * ROWS, ROWS)
        top, scale = peak_ref[rows, :], 1.0 / row_ref[rows, :]
        for t, (k, g, n) in enumerate(tiles):
            x = logits[k][f, g, :, n:n + LANES] + c_ref[:, lanes(where[0, t])]
            out_ref[rows, lanes(where[1, t])] = (jnp.exp(x - top) * scale).astype(jnp.bfloat16)
        return 0

    lax.fori_loop(0, blocks, write, 0)


def row_call(kernel, out_shape, where, logits, c):
    shapes = tuple(a.shape for a in logits)
    rows = shapes[0][0] * ROWS
    vmem = pl.BlockSpec(memory_space=pltpu.VMEM)
    return pl.pallas_call(
        functools.partial(kernel, shapes),
        out_shape=out_shape,
        in_specs=[pl.BlockSpec(memory_space=pltpu.SMEM)] + [vmem] * (len(logits) + 1),
        out_specs=vmem,
        scratch_shapes=[pltpu.VMEM((rows, LANES), jnp.float32)] * 2,
        compiler_params=pltpu.CompilerParams(vmem_limit_bytes=32 * 2**20),
    )(where, *logits, c)


def combine(a, b):
    peak = jnp.maximum(a[0], b[0])
    total = a[1] * jnp.exp(a[0] - peak) + b[1] * jnp.exp(b[0] - peak)
    return jnp.stack([peak, total])


def column_update(stats):
    for axis, n, step in (("core", 2, 1), ("y", 4, 1), ("y", 4, 2), ("zh", 2, 1)):
        pairs = [(i, i ^ step) for i in range(n)]
        stats = combine(stats, lax.ppermute(stats, axis, pairs))
    return -(stats[0] + jnp.log(stats[1]))[None, :]


def lane_sums(x):
    acc = None
    for n in range(0, x.shape[1], LANES):
        v = x[:, n:n + LANES].astype(jnp.float32)
        acc = v * v if acc is None else acc + v * v
    return acc


def partial_kernel(nq, widths, scale, *refs):
    n_refs, x_refs = refs[:nq], refs[nq:nq + len(widths)]
    out_ref, noise_sq, data_sq = refs[nq + len(widths):]
    step = pl.program_id(0)
    rows = n_refs[0].shape[0]
    parts = out_ref.shape[0]
    share = rows // parts

    @pl.when(step == 0)
    def _():
        out_ref[...] = jnp.zeros_like(out_ref)
        noise_sq[...] = jnp.zeros_like(noise_sq)
        data_sq[...] = jnp.zeros_like(data_sq)

    for q in range(nq):
        block = n_refs[q][...]
        noise_sq[q] += lane_sums(block)
        first = 0
        for x, width in zip(x_refs, widths):
            inner = lax.dot_general(
                block, x[...], (((1,), (1,)), ((), ())), preferred_element_type=jnp.float32
            )
            out_ref[:, q, :, first:first + width] += inner.reshape(parts, share, width)
            first += width
    first = 0
    for x, width in zip(x_refs, widths):
        data_sq[first:first + width, :] += lane_sums(x[...])
        first += width

    @pl.when(step == pl.num_programs(0) - 1)
    def _():
        columns = lax.dot_general(
            jnp.ones((8, LANES), jnp.float32), data_sq[...], (((1,), (1,)), ((), ())),
            precision=lax.Precision.HIGHEST, preferred_element_type=jnp.float32,
        )[0:1]
        for q in range(nq):
            square = jnp.sum(noise_sq[q], axis=1, keepdims=True)
            for f in range(parts):
                own = square[f * share:(f + 1) * share]
                out_ref[f, q] = (own + columns - 2.0 * out_ref[f, q]) * scale


def partial_call(scale, parts, noises, datas):
    nq, widths = len(noises), tuple(d.shape[0] for d in datas)
    rows, depth = noises[0].shape
    shape = (parts, nq, rows // parts, sum(widths))
    block = DEPTH
    return pl.pallas_call(
        functools.partial(partial_kernel, nq, widths, scale),
        out_shape=jax.ShapeDtypeStruct(shape, jnp.float32),
        grid=(depth // block,),
        in_specs=[pl.BlockSpec((a.shape[0], block), lambda k: (0, k)) for a in (*noises, *datas)],
        out_specs=pl.BlockSpec(shape, lambda k: (0, 0, 0, 0)),
        scratch_shapes=[
            pltpu.VMEM((nq, rows, LANES), jnp.float32),
            pltpu.VMEM((sum(widths), LANES), jnp.float32),
        ],
        compiler_params=pltpu.CompilerParams(vmem_limit_bytes=48 * 2**20),
    )(*noises, *datas)


def targets_kernel(widths, w_ref, *refs):
    x_refs, out_ref = refs[:-1], refs[-1]
    first, acc = 0, None
    for x, width in zip(x_refs, widths):
        part = jnp.dot(w_ref[:, first:first + width], x[...], preferred_element_type=jnp.float32)
        acc = part if acc is None else acc + part
        first += width
    out_ref[...] = acc.astype(out_ref.dtype)


def targets_call(weights, datas):
    widths = tuple(d.shape[0] for d in datas)
    rows, depth = weights.shape[0], datas[0].shape[1]
    block = 512
    return pl.pallas_call(
        functools.partial(targets_kernel, widths),
        out_shape=jax.ShapeDtypeStruct((rows, depth), jnp.bfloat16),
        grid=(depth // block,),
        in_specs=[pl.BlockSpec(weights.shape, lambda n: (0, 0))]
        + [pl.BlockSpec((w, block), lambda n: (0, n)) for w in widths],
        out_specs=pl.BlockSpec((rows, block), lambda n: (0, n)),
        compiler_params=pltpu.CompilerParams(vmem_limit_bytes=48 * 2**20),
    )(weights, *datas)


def ring(x, shift):
    return lax.ppermute(x, "y", [(i, (i + shift) % 4) for i in range(4)])


def swap(x, dz, dc):
    if dz and dc:
        return lax.ppermute(x, ("zh", "core"), [(i, 3 - i) for i in range(4)])
    if dz or dc:
        return lax.ppermute(x, "zh" if dz else "core", [(0, 1), (1, 0)])
    return x


def ring_gather(x):
    half = x.shape[0] // 2
    a, b = x[:half], x[half:]
    u1, w1 = ring(a, 1), ring(a, -1)
    u2, w2 = ring(b, 1), ring(b, -1)
    u3, w3 = ring(u1, 1), ring(w2, -1)
    return [x, u1, w1, u2, w2, u3, w3]


SOURCES = [(0, 0), (0, 1), (-1, 0), (1, 0), (-1, 1), (1, 1), (-2, 0), (2, 1)]
QUARTERS = [(0, 0), (0, 1), (1, 0), (1, 1)]


def sum_and_share(part, quarters):
    own = lax.psum_scatter(part, FEAT, scatter_dimension=0, tiled=False)
    own = jnp.stack([swap(own[i], *q) for i, q in enumerate(quarters)])
    return lax.all_gather(own, FEAT, axis=0, tiled=False)


def tables(chunks):
    zh, y, core = (lax.axis_index(a) for a in ("zh", "y", "core"))
    where, place = [], []
    for quarters, sources in chunks:
        for dz, dc in quarters:
            for s in sources:
                dy, half = SOURCES[s]
                inside = ((y + dy + 4) % 4 * 2 + (core + dc) % 2) * 2 + half
                where.append((zh + dz) % 2 * 16 + inside)
                place.append(16 + inside if dz else jnp.int32(dc * 8 + s))
    return jnp.stack([jnp.stack(where), jnp.stack(place)]).astype(jnp.int32)


def local(noise, data):
    temper = 0.5 / math.sqrt(F)
    scale = -1.0 / (F * temper)
    parts = 8
    near = [noise, swap(noise, 0, 1)]
    far = swap(noise, 1, 0)
    blocks = ring_gather(data)
    far = [far, swap(far, 0, 1)]
    data, far[0] = lax.optimization_barrier((data, far[0]))
    other = swap(data, 1, 0)

    first, second, third = blocks[:3], blocks[3:5], blocks[5:]
    everyone = near + far
    p1 = partial_call(scale, parts, near, first)
    p2 = partial_call(scale, parts, far, first)
    p3 = partial_call(scale, parts, everyone, second)
    p4 = partial_call(scale, parts, everyone, third)
    chunks = [
        (QUARTERS[:2], (0, 1, 2, 3)),
        (QUARTERS[2:], (0, 1, 2, 3)),
        (QUARTERS, (4, 5)),
        (QUARTERS, (6, 7)),
    ]
    logits = [sum_and_share(p, q) for p, (q, _) in zip((p1, p2, p3, p4), chunks)]
    where = tables(chunks)

    others = lax.all_gather(other, ("y", "core"), axis=0, tiled=True)
    gathered = blocks + [swap(b, 0, 1) for b in blocks] + [others]

    c = jnp.zeros((1, SAMPLES), jnp.float32)
    for _ in range(ITERS):
        out = jax.ShapeDtypeStruct((2, SAMPLES), jnp.float32)
        c = column_update(row_call(sinkhorn_kernel, out, where, logits, c))
    out = jax.ShapeDtypeStruct((noise.shape[0], SAMPLES), jnp.bfloat16)
    weights = row_call(weights_kernel, out, where, logits, c)
    share = SAMPLES // parts
    start = (lax.axis_index("zl") * 4 + lax.axis_index("x")) * share
    column_out = lax.dynamic_slice_in_dim(c[0] * temper, start, share, 0)
    return (targets_call(weights, gathered), column_out)


def solution(mesh):
    fine = Mesh(mesh.devices.reshape(2, 4, 2, 2, 4), ("zh", "y", "core", "zl", "x"))
    samp, feat = ("zh", "y", "core"), FEAT
    in_specs = (P(samp, feat), P(samp, feat))
    out_specs = (P(samp, feat), P(feat))
    return jax.shard_map(local, mesh=fine, in_specs=in_specs, out_specs=out_specs, check_vma=False)
```

```python
import functools
import math

import jax
import jax.numpy as jnp
from jax import lax
from jax.experimental import pallas as pl
from jax.experimental.pallas import tpu as pltpu
from jax.sharding import Mesh, PartitionSpec as P

F = 32768
ITERS = 3
SAMPLES = 4096
LANES = 128
ROWS = 32
GROUP = 4
SPREAD = 2
DEPTH = 1024
FEAT = ("zl", "x")


def tile_list(shapes):
    return [
        (k, g, n)
        for k, (_, groups, _, width) in enumerate(shapes)
        for g in range(groups)
        for n in range(0, width, LANES)
    ]


def row_pass(tiles, blocks, logits, where, c_ref, peak_ref, row_ref):
    def tile(f, t):
        k, g, n = tiles[t]
        return logits[k][f, g, :, n:n + LANES] + c_ref[:, lanes(where[0, t])]

    def maxima(f, _):
        acc = tile(f, 0)
        for t in range(1, len(tiles)):
            acc = jnp.maximum(acc, tile(f, t))
        peak_ref[pl.ds(f * ROWS, ROWS), :] = acc
        return 0

    lax.fori_loop(0, blocks, maxima, 0)
    peak = jnp.max(peak_ref[...], axis=1, keepdims=True)
    peak_ref[...] = jnp.broadcast_to(peak, peak_ref.shape)

    def totals(f, _):
        top = peak_ref[pl.ds(f * ROWS, ROWS), :]
        acc = jnp.exp(tile(f, 0) - top)
        for t in range(1, len(tiles)):
            acc = acc + jnp.exp(tile(f, t) - top)
        row_ref[pl.ds(f * ROWS, ROWS), :] = acc
        return 0

    lax.fori_loop(0, blocks, totals, 0)
    return jnp.sum(row_ref[...], axis=1, keepdims=True)


def lanes(tile):
    return pl.ds(pl.multiple_of(tile * LANES, LANES), LANES)


def sinkhorn_kernel(shapes, where, *refs):
    logits, (c_ref, out_ref, peak_ref, row_ref) = refs[:len(shapes)], refs[len(shapes):]
    tiles = tile_list(shapes)
    blocks = shapes[0][0]
    total = row_pass(tiles, blocks, logits, where, c_ref, peak_ref, row_ref)
    row_ref[...] = jnp.broadcast_to(-(peak_ref[:, 0:1] + jnp.log(total)), row_ref.shape)
    for first in range(0, len(tiles), GROUP):
        group = range(first, first + GROUP)

        def values(f, r, t):
            k, g, n = tiles[t]
            rows = row_ref[pl.ds(f * ROWS + r * 8, 8), :]
            return logits[k][f, g, r * 8:(r + 1) * 8, n:n + LANES] + rows

        def maxima(f, acc):
            for r in range(ROWS // 8):
                acc = [jnp.maximum(a, values(f, r, t)) for a, t in zip(acc, group)]
            return acc

        start = [jnp.full((8, LANES), -jnp.inf, jnp.float32) for _ in group]
        acc = lax.fori_loop(0, blocks, maxima, start)
        peaks = [jnp.max(a, axis=0, keepdims=True) for a in acc]

        def totals(f, acc):
            for r in range(ROWS // 8):
                acc = [a + jnp.exp(values(f, r, t) - p) for a, p, t in zip(acc, peaks, group)]
            return acc

        start = [jnp.zeros((8, LANES), jnp.float32) for _ in group]
        acc = lax.fori_loop(0, blocks, totals, start)
        for a, p, t in zip(acc, peaks, group):
            out_ref[0:1, lanes(where[0, t])] = p
            out_ref[1:2, lanes(where[0, t])] = jnp.sum(a, axis=0, keepdims=True)


def weights_kernel(shapes, where, *refs):
    logits, (c_ref, out_ref, peak_ref, row_ref) = refs[:len(shapes)], refs[len(shapes):]
    tiles = tile_list(shapes)
    blocks = shapes[0][0]
    total = row_pass(tiles, blocks, logits, where, c_ref, peak_ref, row_ref)
    row_ref[...] = jnp.broadcast_to(total, row_ref.shape)

    def write(f, _):
        rows = pl.ds(f * ROWS, ROWS)
        top, scale = peak_ref[rows, :], 1.0 / row_ref[rows, :]
        for t, (k, g, n) in enumerate(tiles):
            x = logits[k][f, g, :, n:n + LANES] + c_ref[:, lanes(where[0, t])]
            out_ref[rows, lanes(where[1, t])] = (jnp.exp(x - top) * scale).astype(jnp.bfloat16)
        return 0

    lax.fori_loop(0, blocks, write, 0)


def row_call(kernel, out_shape, where, logits, c):
    shapes = tuple(a.shape for a in logits)
    rows = shapes[0][0] * ROWS
    vmem = pl.BlockSpec(memory_space=pltpu.VMEM)
    return pl.pallas_call(
        functools.partial(kernel, shapes),
        out_shape=out_shape,
        in_specs=[pl.BlockSpec(memory_space=pltpu.SMEM)] + [vmem] * (len(logits) + 1),
        out_specs=vmem,
        scratch_shapes=[pltpu.VMEM((rows, LANES), jnp.float32)] * 2,
        compiler_params=pltpu.CompilerParams(vmem_limit_bytes=32 * 2**20),
    )(where, *logits, c)


def combine(a, b):
    peak = jnp.maximum(a[0], b[0])
    total = a[1] * jnp.exp(a[0] - peak) + b[1] * jnp.exp(b[0] - peak)
    return jnp.stack([peak, total])


SAMP_STEPS = (("core", 2, 1), ("y", 4, 1), ("y", 4, 2), ("zh", 2, 1))
FEAT_STEPS = (("zl", 2, 1), ("x", 4, 1), ("x", 4, 2))


def column_update(stats, steps):
    for axis, n, step in steps:
        pairs = [(i, i ^ step) for i in range(n)]
        stats = combine(stats, lax.ppermute(stats, axis, pairs))
    return -(stats[0] + jnp.log(stats[1]))[None, :]


def lane_sums(x):
    acc = None
    for n in range(0, x.shape[1], LANES):
        v = x[:, n:n + LANES].astype(jnp.float32)
        acc = v * v if acc is None else acc + v * v
    return acc


def partial_kernel(jobs, scale, *refs):
    n_count = 1 + max(q for qs, _ in jobs for q in qs)
    x_count = 1 + max(x for _, xs in jobs for x in xs)
    where, refs = refs[0], refs[1:]
    n_refs, n_sq, x_refs = refs[:n_count], refs[n_count:2 * n_count], refs[2 * n_count:2 * n_count + x_count]
    outs, (acc, x_sq) = refs[2 * n_count + x_count:-2], refs[-2:]
    step = pl.program_id(0)
    rows = n_refs[0].shape[0]
    parts, share, _ = acc.shape

    @pl.when(step == 0)
    def _():
        acc[...] = jnp.zeros_like(acc)
        x_sq[...] = jnp.zeros_like(x_sq)

    places, first = [], 0
    for qs, xs in jobs:
        widths = [x_refs[x].shape[0] for x in xs]
        block = jnp.concatenate([n_refs[q][...] for q in qs], axis=0)
        offset = first
        for x, width in zip(xs, widths):
            inner = lax.dot_general(
                block, x_refs[x][...], (((1,), (1,)), ((), ())), preferred_element_type=jnp.float32
            )
            for i, q in enumerate(qs):
                at = offset + i * sum(widths)
                part = inner[i * rows:(i + 1) * rows].reshape(parts, share, width)
                acc[:, :, at:at + width] += part
                places.append((q, x, at))
            offset += width
        first += len(qs) * sum(widths)
    starts = [sum(r.shape[0] for r in x_refs[:x]) for x in range(x_count)]
    for x, start in zip(x_refs, starts):
        x_sq[start:start + x.shape[0], :] += lane_sums(x[...])

    @pl.when(step == pl.num_programs(0) - 1)
    def _():
        columns = lax.dot_general(
            jnp.ones((8, LANES), jnp.float32), x_sq[...], (((1,), (1,)), ((), ())),
            precision=lax.Precision.HIGHEST, preferred_element_type=jnp.float32,
        )[0:1]
        for d, out in zip((0, 1, -1, 2), outs):
            for z in range(2):
                f = (where[1] + z) % 2 * 4 + (where[0] + d + 4) % 4
                for q, x, at in places:
                    width = x_refs[x].shape[0]
                    own = n_sq[q][pl.ds(f * share, share), :]
                    other = columns[:, starts[x]:starts[x] + width]
                    inner = acc[f, :, at:at + width]
                    out[z, :, at:at + width] = (own + other - 2.0 * inner) * scale


def partial_call(scale, parts, where, noises, squares, datas, jobs):
    rows, depth = noises[0].shape
    total = sum(len(qs) * sum(datas[x].shape[0] for x in xs) for qs, xs in jobs)
    share = rows // parts
    block = DEPTH
    out = (2, share, total)
    return pl.pallas_call(
        functools.partial(partial_kernel, jobs, scale),
        out_shape=[jax.ShapeDtypeStruct(out, jnp.float32)] * 4,
        grid=(depth // block,),
        in_specs=[pl.BlockSpec(memory_space=pltpu.SMEM)]
        + [pl.BlockSpec((rows, block), lambda k: (0, k)) for _ in noises]
        + [pl.BlockSpec((rows, 1), lambda k: (0, 0)) for _ in noises]
        + [pl.BlockSpec((d.shape[0], block), lambda k: (0, k)) for d in datas],
        out_specs=[pl.BlockSpec(out, lambda k: (0, 0, 0))] * 4,
        scratch_shapes=[
            pltpu.VMEM((parts, share, total), jnp.float32),
            pltpu.VMEM((sum(d.shape[0] for d in datas), LANES), jnp.float32),
        ],
        compiler_params=pltpu.CompilerParams(vmem_limit_bytes=48 * 2**20),
    )(where, *noises, *squares, *datas)


def targets_kernel(widths, w_ref, *refs):
    x_refs, out_ref = refs[:-1], refs[-1]
    first, acc = 0, None
    for x, width in zip(x_refs, widths):
        part = jnp.dot(w_ref[:, first:first + width], x[...], preferred_element_type=jnp.float32)
        acc = part if acc is None else acc + part
        first += width
    out_ref[...] = acc.astype(out_ref.dtype)


def targets_call(weights, datas):
    widths = tuple(d.shape[0] for d in datas)
    rows, depth = weights.shape[0], datas[0].shape[1]
    block = 512
    return pl.pallas_call(
        functools.partial(targets_kernel, widths),
        out_shape=jax.ShapeDtypeStruct((rows, depth), jnp.bfloat16),
        grid=(depth // block,),
        in_specs=[pl.BlockSpec(weights.shape, lambda n: (0, 0))]
        + [pl.BlockSpec((w, block), lambda n: (0, n)) for w in widths],
        out_specs=pl.BlockSpec((rows, block), lambda n: (0, n)),
        compiler_params=pltpu.CompilerParams(vmem_limit_bytes=48 * 2**20),
    )(weights, *datas)


def ring(x, shift):
    return lax.ppermute(x, "y", [(i, (i + shift) % 4) for i in range(4)])


def swap(x, dz, dc):
    if dz and dc:
        return lax.ppermute(x, ("zh", "core"), [(i, 3 - i) for i in range(4)])
    if dz or dc:
        return lax.ppermute(x, "zh" if dz else "core", [(0, 1), (1, 0)])
    return x


def ring_gather(x):
    half = x.shape[0] // 2
    a, b = x[:half], x[half:]
    u1, w1 = ring(a, 1), ring(a, -1)
    u2, w2 = ring(b, 1), ring(b, -1)
    u3, w3 = ring(u1, 1), ring(w2, -1)
    return [x, u1, w1, u2, w2, u3, w3]


SOURCES = [(0, 0), (0, 1), (-1, 0), (1, 0), (-1, 1), (1, 1), (-2, 0), (2, 1)]
QUARTERS = [(0, 0), (0, 1), (1, 0), (1, 1)]


def sum_over_feat(pieces):
    own, right, left, across = pieces
    for piece, step in ((right, 1), (left, -1), (across, 2)):
        own = own + lax.ppermute(piece, "x", [(i, (i + step) % 4) for i in range(4)])
    return own[0] + lax.ppermute(own[1], "zl", [(0, 1), (1, 0)])


def tables(parts):
    zh, y, core = (lax.axis_index(a) for a in ("zh", "y", "core"))
    where, place = [], []
    for dz, dc in QUARTERS:
        for s, (dy, half) in enumerate(SOURCES):
            inside = ((y + dy + 4) % 4 * 2 + (core + dc) % 2) * 2 + half
            where.append((zh + dz) % 2 * 16 + inside)
            place.append(16 + inside if dz else jnp.int32(dc * 8 + s))
    return jnp.stack([jnp.stack(where), jnp.stack(place)]).astype(jnp.int32)


def row_squares(x):
    return jnp.sum(jnp.square(x.astype(jnp.float32)), axis=1, keepdims=True)


def local(noise, data):
    temper = 0.5 / math.sqrt(F)
    scale = -1.0 / (F * temper)
    parts = 8
    near = [noise, swap(noise, 0, 1)]
    far = swap(noise, 1, 0)
    blocks = ring_gather(data)
    far = [far, swap(far, 0, 1)]
    data, far[0] = lax.optimization_barrier((data, far[0]))
    other = swap(data, 1, 0)

    everyone = near + far
    squares = [row_squares(n) for n in everyone]
    here = jnp.stack([lax.axis_index("x"), lax.axis_index("zl")]).astype(jnp.int32)
    call = functools.partial(partial_call, scale, parts, here)
    pieces = call(near, squares[:2], blocks[:3], (((0, 1), (0, 1, 2)),))
    sum1 = sum_over_feat(pieces)
    pieces = call(everyone, squares, blocks[:5], (((2, 3), (0, 1, 2)), ((0, 1, 2, 3), (3, 4))))
    sum2 = sum_over_feat(pieces)
    pieces = call(everyone, squares, blocks[5:], (((0, 1, 2, 3), (0, 1)),))
    sum3 = sum_over_feat(pieces)
    quarters = []
    for i, q in enumerate(QUARTERS):
        head = sum2[:, (i - 2) * 512:(i - 1) * 512] if i >= 2 else sum1[:, i * 512:(i + 1) * 512]
        middle = sum2[:, 1024 + i * 256:1280 + i * 256]
        quarters.append(swap(jnp.concatenate([head, middle, sum3[:, i * 256:(i + 1) * 256]], axis=1), *q))
    own = jnp.stack(quarters)
    where = tables(parts)

    shared = lax.all_gather(own, FEAT, axis=0, tiled=False)
    others = lax.all_gather(other, ("y", "core"), axis=0, tiled=True)
    gathered = blocks + [swap(b, 0, 1) for b in blocks] + [others]

    c = jnp.zeros((1, SAMPLES), jnp.float32)
    for i in range(ITERS):
        out = jax.ShapeDtypeStruct((2, SAMPLES), jnp.float32)
        if i < SPREAD:
            c = column_update(row_call(sinkhorn_kernel, out, where, [own[None]], c), SAMP_STEPS + FEAT_STEPS)
        else:
            c = column_update(row_call(sinkhorn_kernel, out, where, [shared], c), SAMP_STEPS)
    out = jax.ShapeDtypeStruct((noise.shape[0], SAMPLES), jnp.bfloat16)
    weights = row_call(weights_kernel, out, where, [shared], c)
    share = SAMPLES // parts
    start = (lax.axis_index("zl") * 4 + lax.axis_index("x")) * share
    column_out = lax.dynamic_slice_in_dim(c[0] * temper, start, share, 0)
    return (targets_call(weights, gathered), column_out)


def solution(mesh):
    fine = Mesh(mesh.devices.reshape(2, 4, 2, 2, 4), ("zh", "y", "core", "zl", "x"))
    samp, feat = ("zh", "y", "core"), FEAT
    in_specs = (P(samp, feat), P(samp, feat))
    out_specs = (P(samp, feat), P(feat))
    return jax.shard_map(local, mesh=fine, in_specs=in_specs, out_specs=out_specs, check_vma=False)
```

```python
import functools
import math

import jax
import jax.numpy as jnp
from jax import lax
from jax.experimental import pallas as pl
from jax.experimental.pallas import tpu as pltpu
from jax.sharding import Mesh, PartitionSpec as P

F = 32768
ITERS = 3
SAMPLES = 4096
LANES = 128
ROWS = 32
GROUP = 4
SPREAD = 2
DEPTH = 1024
FEAT = ("zl", "x")


def tile_list(shapes):
    return [
        (k, g, n)
        for k, (_, groups, _, width) in enumerate(shapes)
        for g in range(groups)
        for n in range(0, width, LANES)
    ]


def row_pass(tiles, blocks, logits, where, c_ref, peak_ref, row_ref):
    def tile(f, t):
        k, g, n = tiles[t]
        return logits[k][f, g, :, n:n + LANES] + c_ref[:, lanes(where[0, t])]

    def maxima(f, _):
        acc = tile(f, 0)
        for t in range(1, len(tiles)):
            acc = jnp.maximum(acc, tile(f, t))
        peak_ref[pl.ds(f * ROWS, ROWS), :] = acc
        return 0

    lax.fori_loop(0, blocks, maxima, 0)
    peak = jnp.max(peak_ref[...], axis=1, keepdims=True)
    peak_ref[...] = jnp.broadcast_to(peak, peak_ref.shape)

    def totals(f, _):
        top = peak_ref[pl.ds(f * ROWS, ROWS), :]
        acc = jnp.exp(tile(f, 0) - top)
        for t in range(1, len(tiles)):
            acc = acc + jnp.exp(tile(f, t) - top)
        row_ref[pl.ds(f * ROWS, ROWS), :] = acc
        return 0

    lax.fori_loop(0, blocks, totals, 0)
    return jnp.sum(row_ref[...], axis=1, keepdims=True)


def lanes(tile):
    return pl.ds(pl.multiple_of(tile * LANES, LANES), LANES)


def sinkhorn_kernel(shapes, where, *refs):
    logits, (c_ref, out_ref, peak_ref, row_ref) = refs[:len(shapes)], refs[len(shapes):]
    tiles = tile_list(shapes)
    blocks = shapes[0][0]
    total = row_pass(tiles, blocks, logits, where, c_ref, peak_ref, row_ref)
    row_ref[...] = jnp.broadcast_to(-(peak_ref[:, 0:1] + jnp.log(total)), row_ref.shape)
    for first in range(0, len(tiles), GROUP):
        group = range(first, first + GROUP)

        def values(f, r, t):
            k, g, n = tiles[t]
            rows = row_ref[pl.ds(f * ROWS + r * 8, 8), :]
            return logits[k][f, g, r * 8:(r + 1) * 8, n:n + LANES] + rows

        def maxima(f, acc):
            for r in range(ROWS // 8):
                acc = [jnp.maximum(a, values(f, r, t)) for a, t in zip(acc, group)]
            return acc

        start = [jnp.full((8, LANES), -jnp.inf, jnp.float32) for _ in group]
        acc = lax.fori_loop(0, blocks, maxima, start)
        peaks = [jnp.max(a, axis=0, keepdims=True) for a in acc]

        def totals(f, acc):
            for r in range(ROWS // 8):
                acc = [a + jnp.exp(values(f, r, t) - p) for a, p, t in zip(acc, peaks, group)]
            return acc

        start = [jnp.zeros((8, LANES), jnp.float32) for _ in group]
        acc = lax.fori_loop(0, blocks, totals, start)
        for a, p, t in zip(acc, peaks, group):
            out_ref[0:1, lanes(where[0, t])] = p
            out_ref[1:2, lanes(where[0, t])] = jnp.sum(a, axis=0, keepdims=True)


def exponentials_kernel(shapes, where, *refs):
    logits, (c_ref, out_ref, peak_ref, _) = refs[:len(shapes)], refs[len(shapes):]
    tiles = tile_list(shapes)
    acc = None
    for t, (k, g, n) in enumerate(tiles):
        x = logits[k][0, g, :, n:n + LANES] + c_ref[:, lanes(where[0, t])]
        acc = x if acc is None else jnp.maximum(acc, x)
    peak_ref[...] = jnp.broadcast_to(jnp.max(acc, axis=1, keepdims=True), peak_ref.shape)
    top = peak_ref[...]
    for t, (k, g, n) in enumerate(tiles):
        x = logits[k][0, g, :, n:n + LANES] + c_ref[:, lanes(where[0, t])]
        out_ref[g, :, n:n + LANES] = jnp.exp(x - top).astype(jnp.bfloat16)


def scaled_rows(tiles, kernels, where, v_ref, row_ref):
    for d, k_ref in enumerate(kernels):
        for z in range(k_ref.shape[0]):
            acc = None
            for t, (_, g, n) in enumerate(tiles):
                x = k_ref[z, g, :, n:n + LANES].astype(jnp.float32) * v_ref[:, lanes(where[0, t])]
                acc = x if acc is None else acc + x
            first = (d * k_ref.shape[0] + z) * ROWS
            row_ref[first:first + ROWS, :] = acc
    return jnp.sum(row_ref[...], axis=1, keepdims=True)


def balance_kernel(shapes, where, *refs):
    kernels, (v_ref, out_ref, row_ref) = refs[:len(shapes)], refs[len(shapes):]
    tiles = tile_list(((1,) + shapes[0][1:],))
    total = scaled_rows(tiles, kernels, where, v_ref, row_ref)
    row_ref[...] = jnp.broadcast_to(1.0 / total, row_ref.shape)
    for t, (_, g, n) in enumerate(tiles):
        acc = jnp.zeros((ROWS, LANES), jnp.float32)
        for d, k_ref in enumerate(kernels):
            for z in range(k_ref.shape[0]):
                first = (d * k_ref.shape[0] + z) * ROWS
                acc = acc + k_ref[z, g, :, n:n + LANES].astype(jnp.float32) * row_ref[first:first + ROWS, :]
        out_ref[0:1, lanes(where[0, t])] = jnp.sum(acc, axis=0, keepdims=True)


def weights_kernel(shapes, where, *refs):
    kernels, (v_ref, out_ref, row_ref) = refs[:len(shapes)], refs[len(shapes):]
    tiles = tile_list(((1,) + shapes[0][1:],))
    total = scaled_rows(tiles, kernels, where, v_ref, row_ref)
    row_ref[...] = jnp.broadcast_to(1.0 / total, row_ref.shape)
    for d, k_ref in enumerate(kernels):
        for z in range(k_ref.shape[0]):
            first = (d * k_ref.shape[0] + z) * ROWS
            scale = row_ref[first:first + ROWS, :]
            rows = pl.ds(pl.multiple_of(where[2, d * k_ref.shape[0] + z] * ROWS, ROWS), ROWS)
            for t, (_, g, n) in enumerate(tiles):
                x = k_ref[z, g, :, n:n + LANES].astype(jnp.float32) * v_ref[:, lanes(where[0, t])]
                out_ref[rows, lanes(where[1, t])] = (x * scale).astype(jnp.bfloat16)


def balance_call(kernel, out_shape, where, kernels, v):
    shapes = tuple(a.shape for a in kernels)
    rows = sum(s[0] for s in shapes) * ROWS
    vmem = pl.BlockSpec(memory_space=pltpu.VMEM)
    return pl.pallas_call(
        functools.partial(kernel, shapes),
        out_shape=out_shape,
        in_specs=[pl.BlockSpec(memory_space=pltpu.SMEM)] + [vmem] * (len(kernels) + 1),
        out_specs=vmem,
        scratch_shapes=[pltpu.VMEM((rows, LANES), jnp.float32)],
        compiler_params=pltpu.CompilerParams(vmem_limit_bytes=32 * 2**20),
    )(where, *kernels, v)


def row_call(kernel, out_shape, where, logits, c):
    shapes = tuple(a.shape for a in logits)
    rows = shapes[0][0] * ROWS
    vmem = pl.BlockSpec(memory_space=pltpu.VMEM)
    return pl.pallas_call(
        functools.partial(kernel, shapes),
        out_shape=out_shape,
        in_specs=[pl.BlockSpec(memory_space=pltpu.SMEM)] + [vmem] * (len(logits) + 1),
        out_specs=vmem,
        scratch_shapes=[pltpu.VMEM((rows, LANES), jnp.float32)] * 2,
        compiler_params=pltpu.CompilerParams(vmem_limit_bytes=32 * 2**20),
    )(where, *logits, c)


def combine(a, b):
    peak = jnp.maximum(a[0], b[0])
    total = a[1] * jnp.exp(a[0] - peak) + b[1] * jnp.exp(b[0] - peak)
    return jnp.stack([peak, total])


SAMP_STEPS = (("core", 2, 1), ("y", 4, 1), ("y", 4, 2), ("zh", 2, 1))
FEAT_STEPS = (("zl", 2, 1), ("x", 4, 1), ("x", 4, 2))


def column_sum(x):
    for axis, n, step in SAMP_STEPS:
        x = x + lax.ppermute(x, axis, [(i, i ^ step) for i in range(n)])
    return x


def column_update(stats, steps):
    for axis, n, step in steps:
        pairs = [(i, i ^ step) for i in range(n)]
        stats = combine(stats, lax.ppermute(stats, axis, pairs))
    return -(stats[0] + jnp.log(stats[1]))[None, :]


def lane_sums(x):
    acc = None
    for n in range(0, x.shape[1], LANES):
        v = x[:, n:n + LANES].astype(jnp.float32)
        acc = v * v if acc is None else acc + v * v
    return acc


def partial_kernel(noise_parts, jobs, scale, *refs):
    n_count = sum(noise_parts)
    x_count = 1 + max(x for _, xs in jobs for x in xs)
    where, n_sq = refs[0], refs[1]
    n_refs, x_refs = refs[2:2 + n_count], refs[2 + n_count:2 + n_count + x_count]
    outs, (acc, x_sq) = refs[2 + n_count + x_count:-2], refs[-2:]
    step = pl.program_id(0)
    parts, share, _ = acc.shape
    rows = parts * share
    starts = [sum(noise_parts[:q]) for q in range(len(noise_parts))]

    @pl.when(step == 0)
    def _():
        acc[...] = jnp.zeros_like(acc)
        x_sq[...] = jnp.zeros_like(x_sq)

    places, first = [], 0
    for qs, xs in jobs:
        widths = [x_refs[x].shape[0] for x in xs]
        block = jnp.concatenate(
            [n_refs[starts[q] + p][...] for q in qs for p in range(noise_parts[q])], axis=0
        )
        offset = first
        for x, width in zip(xs, widths):
            inner = lax.dot_general(
                block, x_refs[x][...], (((1,), (1,)), ((), ())), preferred_element_type=jnp.float32
            )
            for i, q in enumerate(qs):
                at = offset + i * sum(widths)
                part = inner[i * rows:(i + 1) * rows].reshape(parts, share, width)
                acc[:, :, at:at + width] += part
                places.append((q, x, at))
            offset += width
        first += len(qs) * sum(widths)
    x_starts = [sum(r.shape[0] for r in x_refs[:x]) for x in range(x_count)]
    for x, start in zip(x_refs, x_starts):
        x_sq[start:start + x.shape[0], :] += lane_sums(x[...])

    @pl.when(step == pl.num_programs(0) - 1)
    def _():
        columns = lax.dot_general(
            jnp.ones((8, LANES), jnp.float32), x_sq[...], (((1,), (1,)), ((), ())),
            precision=lax.Precision.HIGHEST, preferred_element_type=jnp.float32,
        )[0:1]
        for d, out in zip((0, 1, -1, 2), outs):
            for z in range(2):
                f = (where[1] + z) % 2 * 4 + (where[0] + d + 4) % 4
                for q, x, at in places:
                    width = x_refs[x].shape[0]
                    own = n_sq[pl.ds(q * rows + f * share, share), :]
                    other = columns[:, x_starts[x]:x_starts[x] + width]
                    inner = acc[f, :, at:at + width]
                    out[z, :, at:at + width] = (own + other - 2.0 * inner) * scale


def partial_call(scale, parts, where, squares, noises, datas, jobs):
    noise_parts = tuple(len(n) for n in noises)
    flat = [a for n in noises for a in n]
    rows, depth = sum(a.shape[0] for a in noises[0]), flat[0].shape[1]
    total = sum(len(qs) * sum(datas[x].shape[0] for x in xs) for qs, xs in jobs)
    share = rows // parts
    block = DEPTH
    out = (2, share, total)
    return pl.pallas_call(
        functools.partial(partial_kernel, noise_parts, jobs, scale),
        cost_estimate=pl.CostEstimate(flops=0, bytes_accessed=0, transcendentals=0),
        out_shape=[jax.ShapeDtypeStruct(out, jnp.float32)] * 4,
        grid=(depth // block,),
        in_specs=[pl.BlockSpec(memory_space=pltpu.SMEM)]
        + [pl.BlockSpec(squares.shape, lambda k: (0, 0))]
        + [pl.BlockSpec((a.shape[0], block), lambda k: (0, k)) for a in (*flat, *datas)],
        out_specs=[pl.BlockSpec(out, lambda k: (0, 0, 0))] * 4,
        scratch_shapes=[
            pltpu.VMEM((parts, share, total), jnp.float32),
            pltpu.VMEM((sum(d.shape[0] for d in datas), LANES), jnp.float32),
        ],
        compiler_params=pltpu.CompilerParams(vmem_limit_bytes=48 * 2**20),
    )(where, squares, *flat, *datas)


def targets_kernel(widths, w_ref, *refs):
    x_refs, out_ref = refs[:-1], refs[-1]
    first, acc = 0, None
    for x, width in zip(x_refs, widths):
        part = jnp.dot(w_ref[:, first:first + width], x[...], preferred_element_type=jnp.float32)
        acc = part if acc is None else acc + part
        first += width
    out_ref[...] = acc.astype(out_ref.dtype)


def targets_call(weights, datas):
    widths = tuple(d.shape[0] for d in datas)
    rows, depth = weights.shape[0], datas[0].shape[1]
    block = 512
    return pl.pallas_call(
        functools.partial(targets_kernel, widths),
        out_shape=jax.ShapeDtypeStruct((rows, depth), jnp.bfloat16),
        grid=(depth // block,),
        in_specs=[pl.BlockSpec(weights.shape, lambda n: (0, 0))]
        + [pl.BlockSpec((w, block), lambda n: (0, n)) for w in widths],
        out_specs=pl.BlockSpec((rows, block), lambda n: (0, n)),
        compiler_params=pltpu.CompilerParams(vmem_limit_bytes=48 * 2**20),
    )(weights, *datas)


def ring(x, shift):
    return lax.ppermute(x, "y", [(i, (i + shift) % 4) for i in range(4)])


def swap(x, dz, dc):
    if dz and dc:
        return lax.ppermute(x, ("zh", "core"), [(i, 3 - i) for i in range(4)])
    if dz or dc:
        return lax.ppermute(x, "zh" if dz else "core", [(0, 1), (1, 0)])
    return x


SOURCES = [(0, 0), (0, 1), (-1, 0), (-1, 1), (1, 0), (1, 1), (-2, 0), (2, 1)]
ALONG_X = (0, 1, -1, 2)
QUARTERS = [(0, 0), (0, 1), (1, 0), (1, 1)]


def along_x(x, step):
    return lax.ppermute(x, "x", [(i, (i + step) % 4) for i in range(4)])


def tables(parts):
    zh, y, core = (lax.axis_index(a) for a in ("zh", "y", "core"))
    where, place = [], []
    for dz, dc in QUARTERS:
        for s, (dy, half) in enumerate(SOURCES):
            inside = ((y + dy + 4) % 4 * 2 + (core + dc) % 2) * 2 + half
            where.append((zh + dz) % 2 * 16 + inside)
            place.append(16 + inside if dz else jnp.int32(dc * 8 + s))
    x, zl = lax.axis_index("x"), lax.axis_index("zl")
    rows = [(zl + z) % 2 * 4 + (x + d + 4) % 4 for d in ALONG_X for z in range(2)]
    rows = jnp.pad(jnp.stack(rows), (0, len(where) - len(rows)))
    return jnp.stack([jnp.stack(where), jnp.stack(place), rows]).astype(jnp.int32)


def row_squares(x):
    return jnp.sum(jnp.square(x.astype(jnp.float32)), axis=1, keepdims=True)


def local(noise, data):
    temper = 0.5 / math.sqrt(F)
    scale = -1.0 / (F * temper)
    parts = 8
    half = noise.shape[0] // 2
    call = functools.partial(partial_call, scale, parts)
    where = tables(parts)
    here = jnp.stack([lax.axis_index("x"), lax.axis_index("zl")]).astype(jnp.int32)
    hold = lax.optimization_barrier

    near = swap(noise, 0, 1)
    u, w = ring(data, 1), ring(data, -1)
    far = swap(noise, 1, 0)
    squares = jnp.concatenate([row_squares(n) for n in (noise, near)], axis=0)
    u, w, far, data, squares = hold((u, w, far, data, squares))

    u3, w3 = ring(u[:half], 1), ring(w[half:], -1)
    other = swap(data, 1, 0)
    across = swap(far, 0, 1)
    jobs = (((0, 1), (0, 1, 2)),)
    n0, n1, n3, n2 = call(here, squares, [(noise,), (near,)], [data, u, w], jobs)
    n1, n3 = along_x(n1, 1), along_x(n3, -1)
    far_squares = jnp.concatenate([row_squares(n) for n in (far, across)], axis=0)
    f0, f1, f3, f2 = call(here, far_squares, [(far,), (across,)], [data, u, w], jobs)
    n2 = along_x(n2, 2)
    f1, f3 = along_x(f1, 1), along_x(f3, -1)
    u3, w3, n0, n1, n2, n3, f1, f2, f3 = hold((u3, w3, n0, n1, n2, n3, f1, f2, f3))

    squares = jnp.concatenate([squares, far_squares], axis=0)
    everyone = [(noise,), (near,), (far,), (across,)]
    c0, c1, c3, c2 = call(here, squares, everyone, [u3, w3], (((0, 1, 2, 3), (0, 1)),))
    f2 = along_x(f2, 2)
    c1, c3, c2 = along_x(c1, 1), along_x(c3, -1), along_x(c2, 2)
    f2, c1, c2, c3, other = hold((f2, c1, c2, c3, other))
    n, f, c = n0 + n1 + n2 + n3, f0 + f1 + f2 + f3, c0 + c1 + c2 + c3

    def quarters(z):
        wide, thin = 3 * 256, 256
        return jnp.stack([
            jnp.concatenate([
                (n if i < 2 else f)[z][:, i % 2 * wide:(i % 2 + 1) * wide],
                c[z][:, i * thin:(i + 1) * thin],
            ], axis=1)
            for i in range(4)
        ])

    own = quarters(0) + lax.ppermute(quarters(1), "zl", [(0, 1), (1, 0)])
    own = jnp.stack([swap(own[i], *q) for i, q in enumerate(QUARTERS)])
    own, other = hold((own, other))
    others = lax.all_gather(other, ("y", "core"), axis=0, tiled=True)
    out = jax.ShapeDtypeStruct((2, SAMPLES), jnp.float32)

    def spread(_, c):
        return column_update(row_call(sinkhorn_kernel, out, where, [own[None]], c), SAMP_STEPS + FEAT_STEPS)

    c = lax.fori_loop(0, lax.axis_index("x") // 8 + 1, spread, jnp.zeros((1, SAMPLES), jnp.float32))
    out = jax.ShapeDtypeStruct(own.shape, jnp.bfloat16)
    mine = row_call(exponentials_kernel, out, where, [own[None]], c)
    mine = jnp.stack([mine, lax.ppermute(mine, "zl", [(0, 1), (1, 0)])])
    kernels = [mine] + [along_x(mine, -d) for d in ALONG_X[1:]]

    blocks = [data, u, w, u3, w3]
    kernels, blocks = hold((kernels, blocks))
    swapped = [swap(b, 0, 1) for b in blocks]
    v = jnp.ones((1, SAMPLES), jnp.float32)
    for i in range(1, ITERS):
        out = jax.ShapeDtypeStruct((1, SAMPLES), jnp.float32)
        v = 1.0 / column_sum(balance_call(balance_kernel, out, where, kernels, v))
        if i == 1:
            v, swapped = hold((v, swapped))
    out = jax.ShapeDtypeStruct((noise.shape[0], SAMPLES), jnp.bfloat16)
    weights = balance_call(weights_kernel, out, where, kernels, v)
    c = c + jnp.log(v)
    share = SAMPLES // parts
    start = (lax.axis_index("zl") * 4 + lax.axis_index("x")) * share
    column_out = lax.dynamic_slice_in_dim(c[0] * temper, start, share, 0)
    return (targets_call(weights, [*blocks, *swapped, others]), column_out)


def solution(mesh):
    fine = Mesh(mesh.devices.reshape(2, 4, 2, 2, 4), ("zh", "y", "core", "zl", "x"))
    samp, feat = ("zh", "y", "core"), FEAT
    in_specs = (P(samp, feat), P(samp, feat))
    out_specs = (P(samp, feat), P(feat))
    return jax.shard_map(local, mesh=fine, in_specs=in_specs, out_specs=out_specs, check_vma=False)
```

```python
import functools
import math

import jax
import jax.numpy as jnp
from jax import lax
from jax.experimental import pallas as pl
from jax.experimental.pallas import tpu as pltpu
from jax.sharding import Mesh, PartitionSpec as P

F = 32768
ITERS = 3
SAMPLES = 4096
LANES = 128
ROWS = 32
GROUP = 4
DEPTH = 2048
FEAT = ("zl", "x")


def tile_list(shapes):
    return [
        (k, g, n)
        for k, (_, groups, _, width) in enumerate(shapes)
        for g in range(groups)
        for n in range(0, width, LANES)
    ]


def row_pass(tiles, blocks, logits, where, c_ref, peak_ref, row_ref):
    def tile(f, t):
        k, g, n = tiles[t]
        return logits[k][f, g, :, n:n + LANES] + c_ref[:, lanes(where[0, t])]

    def maxima(f, _):
        acc = tile(f, 0)
        for t in range(1, len(tiles)):
            acc = jnp.maximum(acc, tile(f, t))
        peak_ref[pl.ds(f * ROWS, ROWS), :] = acc
        return 0

    lax.fori_loop(0, blocks, maxima, 0)
    peak = jnp.max(peak_ref[...], axis=1, keepdims=True)
    peak_ref[...] = jnp.broadcast_to(peak, peak_ref.shape)

    def totals(f, _):
        top = peak_ref[pl.ds(f * ROWS, ROWS), :]
        acc = jnp.exp(tile(f, 0) - top)
        for t in range(1, len(tiles)):
            acc = acc + jnp.exp(tile(f, t) - top)
        row_ref[pl.ds(f * ROWS, ROWS), :] = acc
        return 0

    lax.fori_loop(0, blocks, totals, 0)
    return jnp.sum(row_ref[...], axis=1, keepdims=True)


def lanes(tile):
    return pl.ds(pl.multiple_of(tile * LANES, LANES), LANES)


def sinkhorn_kernel(shapes, where, *refs):
    logits, (c_ref, out_ref, peak_ref, row_ref) = refs[:len(shapes)], refs[len(shapes):]
    tiles = tile_list(shapes)
    blocks = shapes[0][0]
    total = row_pass(tiles, blocks, logits, where, c_ref, peak_ref, row_ref)
    row_ref[...] = jnp.broadcast_to(-(peak_ref[:, 0:1] + jnp.log(total)), row_ref.shape)
    for first in range(0, len(tiles), GROUP):
        group = range(first, first + GROUP)

        def values(f, r, t):
            k, g, n = tiles[t]
            rows = row_ref[pl.ds(f * ROWS + r * 8, 8), :]
            return logits[k][f, g, r * 8:(r + 1) * 8, n:n + LANES] + rows

        def maxima(f, acc):
            for r in range(ROWS // 8):
                acc = [jnp.maximum(a, values(f, r, t)) for a, t in zip(acc, group)]
            return acc

        start = [jnp.full((8, LANES), -jnp.inf, jnp.float32) for _ in group]
        acc = lax.fori_loop(0, blocks, maxima, start)
        peaks = [jnp.max(a, axis=0, keepdims=True) for a in acc]

        def totals(f, acc):
            for r in range(ROWS // 8):
                acc = [a + jnp.exp(values(f, r, t) - p) for a, p, t in zip(acc, peaks, group)]
            return acc

        start = [jnp.zeros((8, LANES), jnp.float32) for _ in group]
        acc = lax.fori_loop(0, blocks, totals, start)
        for a, p, t in zip(acc, peaks, group):
            out_ref[0:1, lanes(where[0, t])] = p
            out_ref[1:2, lanes(where[0, t])] = jnp.sum(a, axis=0, keepdims=True)


def exponentials_kernel(shapes, where, *refs):
    logits, (c_ref, out_ref, peak_ref, _) = refs[:len(shapes)], refs[len(shapes):]
    tiles = tile_list(shapes)
    acc = None
    for t, (k, g, n) in enumerate(tiles):
        x = logits[k][0, g, :, n:n + LANES] + c_ref[:, lanes(where[0, t])]
        acc = x if acc is None else jnp.maximum(acc, x)
    peak_ref[...] = jnp.broadcast_to(jnp.max(acc, axis=1, keepdims=True), peak_ref.shape)
    top = peak_ref[...]
    for t, (k, g, n) in enumerate(tiles):
        x = logits[k][0, g, :, n:n + LANES] + c_ref[:, lanes(where[0, t])]
        out_ref[g, :, n:n + LANES] = jnp.exp(x - top).astype(jnp.bfloat16)


def scaled_rows(tiles, kernels, where, v_ref, row_ref):
    for d, k_ref in enumerate(kernels):
        for z in range(k_ref.shape[0]):
            acc = None
            for t, (_, g, n) in enumerate(tiles):
                x = k_ref[z, g, :, n:n + LANES].astype(jnp.float32) * v_ref[:, lanes(where[0, t])]
                acc = x if acc is None else acc + x
            first = (d * k_ref.shape[0] + z) * ROWS
            row_ref[first:first + ROWS, :] = acc
    return jnp.sum(row_ref[...], axis=1, keepdims=True)


def balance_kernel(shapes, where, *refs):
    kernels, (v_ref, out_ref, row_ref) = refs[:len(shapes)], refs[len(shapes):]
    tiles = tile_list(((1,) + shapes[0][1:],))
    total = scaled_rows(tiles, kernels, where, v_ref, row_ref)
    row_ref[...] = jnp.broadcast_to(1.0 / total, row_ref.shape)
    for t, (_, g, n) in enumerate(tiles):
        acc = jnp.zeros((ROWS, LANES), jnp.float32)
        for d, k_ref in enumerate(kernels):
            for z in range(k_ref.shape[0]):
                first = (d * k_ref.shape[0] + z) * ROWS
                acc = acc + k_ref[z, g, :, n:n + LANES].astype(jnp.float32) * row_ref[first:first + ROWS, :]
        out_ref[0:1, lanes(where[0, t])] = jnp.sum(acc, axis=0, keepdims=True)


def targets_kernel(shapes, widths, where, *refs):
    n = len(shapes)
    kernels, v_ref, x_refs, (out_ref, row_ref, w_ref) = refs[:n], refs[n], refs[n + 1:-3], refs[-3:]

    @pl.when(pl.program_id(0) == 0)
    def _():
        tiles = tile_list(((1,) + shapes[0][1:],))
        total = scaled_rows(tiles, kernels, where, v_ref, row_ref)
        row_ref[...] = jnp.broadcast_to(1.0 / total, row_ref.shape)
        for d, k_ref in enumerate(kernels):
            for z in range(k_ref.shape[0]):
                first = (d * k_ref.shape[0] + z) * ROWS
                scale = row_ref[first:first + ROWS, :]
                rows = pl.ds(pl.multiple_of(where[2, d * k_ref.shape[0] + z] * ROWS, ROWS), ROWS)
                for t, (_, g, n) in enumerate(tiles):
                    x = k_ref[z, g, :, n:n + LANES].astype(jnp.float32) * v_ref[:, lanes(where[0, t])]
                    w_ref[rows, lanes(where[1, t])] = (x * scale).astype(jnp.bfloat16)

    first, acc = 0, None
    for x, width in zip(x_refs, widths):
        part = jnp.dot(w_ref[:, first:first + width], x[...], preferred_element_type=jnp.float32)
        acc = part if acc is None else acc + part
        first += width
    out_ref[...] = acc.astype(out_ref.dtype)


def targets_call(where, kernels, v, datas):
    shapes = tuple(a.shape for a in kernels)
    rows = sum(s[0] for s in shapes) * ROWS
    widths = tuple(d.shape[0] for d in datas)
    depth, block = datas[0].shape[1], 1024
    vmem = pl.BlockSpec(memory_space=pltpu.VMEM)
    return pl.pallas_call(
        functools.partial(targets_kernel, shapes, widths),
        out_shape=jax.ShapeDtypeStruct((rows, depth), jnp.bfloat16),
        grid=(depth // block,),
        in_specs=[pl.BlockSpec(memory_space=pltpu.SMEM)] + [vmem] * (len(kernels) + 1)
        + [pl.BlockSpec((w, block), lambda n: (0, n)) for w in widths],
        out_specs=pl.BlockSpec((rows, block), lambda n: (0, n)),
        scratch_shapes=[
            pltpu.VMEM((rows, LANES), jnp.float32),
            pltpu.VMEM((rows, sum(widths)), jnp.bfloat16),
        ],
        compiler_params=pltpu.CompilerParams(vmem_limit_bytes=48 * 2**20),
    )(where, *kernels, v, *datas)


def balance_call(kernel, out_shape, where, kernels, v):
    shapes = tuple(a.shape for a in kernels)
    rows = sum(s[0] for s in shapes) * ROWS
    vmem = pl.BlockSpec(memory_space=pltpu.VMEM)
    return pl.pallas_call(
        functools.partial(kernel, shapes),
        out_shape=out_shape,
        in_specs=[pl.BlockSpec(memory_space=pltpu.SMEM)] + [vmem] * (len(kernels) + 1),
        out_specs=vmem,
        scratch_shapes=[pltpu.VMEM((rows, LANES), jnp.float32)],
        compiler_params=pltpu.CompilerParams(vmem_limit_bytes=32 * 2**20),
    )(where, *kernels, v)


def row_call(kernel, out_shape, where, logits, c):
    shapes = tuple(a.shape for a in logits)
    rows = shapes[0][0] * ROWS
    vmem = pl.BlockSpec(memory_space=pltpu.VMEM)
    return pl.pallas_call(
        functools.partial(kernel, shapes),
        out_shape=out_shape,
        in_specs=[pl.BlockSpec(memory_space=pltpu.SMEM)] + [vmem] * (len(logits) + 1),
        out_specs=vmem,
        scratch_shapes=[pltpu.VMEM((rows, LANES), jnp.float32)] * 2,
        compiler_params=pltpu.CompilerParams(vmem_limit_bytes=32 * 2**20),
    )(where, *logits, c)


def combine(a, b):
    peak = jnp.maximum(a[0], b[0])
    total = a[1] * jnp.exp(a[0] - peak) + b[1] * jnp.exp(b[0] - peak)
    return jnp.stack([peak, total])


SAMP_STEPS = (("core", 2, 1), ("y", 4, 1), ("y", 4, 2), ("zh", 2, 1))
FEAT_STEPS = (("zl", 2, 1), ("x", 4, 1), ("x", 4, 2))


def column_sum(x, steps):
    for axis, n, step in steps:
        x = x + lax.ppermute(x, axis, [(i, i ^ step) for i in range(n)])
    return x


def column_update(stats, steps):
    for axis, n, step in steps:
        pairs = [(i, i ^ step) for i in range(n)]
        stats = combine(stats, lax.ppermute(stats, axis, pairs))
    return -(stats[0] + jnp.log(stats[1]))[None, :]


def lane_sums(x):
    acc = None
    for n in range(0, x.shape[1], LANES):
        v = x[:, n:n + LANES].astype(jnp.float32)
        acc = v * v if acc is None else acc + v * v
    return acc


def partial_kernel(noise_parts, jobs, known, scale, *refs):
    n_count = sum(noise_parts)
    x_count = 1 + max(x for _, xs in jobs for x in xs)
    where, old_n, old_x = refs[:3]
    n_refs, x_refs = refs[3:3 + n_count], refs[3 + n_count:3 + n_count + x_count]
    outs, (n_sq, x_row, acc, x_sq) = refs[3 + n_count + x_count:-4], refs[-4:]
    step = pl.program_id(0)
    parts, share, _ = acc.shape
    rows = parts * share
    starts = [sum(noise_parts[:q]) for q in range(len(noise_parts))]

    @pl.when(step == 0)
    def _():
        acc[...] = jnp.zeros_like(acc)
        n_sq[...] = jnp.zeros_like(n_sq)
        x_sq[...] = jnp.zeros_like(x_sq)

    places, first = [], 0
    for qs, xs in jobs:
        widths = [x_refs[x].shape[0] for x in xs]
        block = jnp.concatenate(
            [n_refs[starts[q] + p][...] for q in qs for p in range(noise_parts[q])], axis=0
        )
        others = jnp.concatenate([x_refs[x][...] for x in xs], axis=0)
        inner = lax.dot_general(
            block, others, (((1,), (1,)), ((), ())), preferred_element_type=jnp.float32
        )
        for i, q in enumerate(qs):
            at = first + i * sum(widths)
            part = inner[i * rows:(i + 1) * rows].reshape(parts, share, sum(widths))
            acc[:, :, at:at + sum(widths)] += part
            for x, width in zip(xs, widths):
                places.append((q, x, at))
                at += width
        first += len(qs) * sum(widths)
    x_starts = [sum(r.shape[0] for r in x_refs[:x]) for x in range(x_count)]
    for squares, blocks, seen in ((n_sq, n_refs, known[0]), (x_sq, x_refs, known[1])):
        start = 0
        for r in blocks:
            if start >= seen:
                squares[start:start + r.shape[0], :] += lane_sums(r[...])
            start += r.shape[0]

    @pl.when(step == pl.num_programs(0) - 1)
    def _():
        x_row[...] = lax.dot_general(
            jnp.ones((8, LANES), jnp.float32), x_sq[...], (((1,), (1,)), ((), ())),
            precision=lax.Precision.HIGHEST, preferred_element_type=jnp.float32,
        )[0:1]
        n_sq[...] = jnp.broadcast_to(jnp.sum(n_sq[...], axis=1, keepdims=True), n_sq.shape)
        if known[0]:
            n_sq[0:known[0], :] = old_n[...]
        if known[1]:
            x_row[:, 0:known[1]] = old_x[...]
        for d, out in zip((0, 1, -1, 2), outs):
            for z in range(2):
                f = (where[1] + z) % 2 * 4 + (where[0] + d + 4) % 4
                for q, x, at in places:
                    width = x_refs[x].shape[0]
                    own = n_sq[pl.ds(q * rows + f * share, share), 0:1]
                    other = x_row[:, x_starts[x]:x_starts[x] + width]
                    inner = acc[f, :, at:at + width]
                    out[z, :, at:at + width] = (own + other - 2.0 * inner) * scale


def partial_call(scale, parts, where, noises, datas, jobs, old_n=None, old_x=None):
    known = (0 if old_n is None else old_n.shape[0], 0 if old_x is None else old_x.shape[1])
    old_n = jnp.zeros((8, LANES), jnp.float32) if old_n is None else old_n
    old_x = jnp.zeros((1, LANES), jnp.float32) if old_x is None else old_x
    noise_parts = tuple(len(n) for n in noises)
    flat = [a for n in noises for a in n]
    rows, depth = sum(a.shape[0] for a in noises[0]), flat[0].shape[1]
    total = sum(len(qs) * sum(datas[x].shape[0] for x in xs) for qs, xs in jobs)
    share = rows // parts
    block = DEPTH
    out = (2, share, total)
    n_rows, columns = sum(a.shape[0] for a in flat), sum(d.shape[0] for d in datas)
    squares = [(n_rows, LANES), (1, columns)]
    *pieces, n_sq, x_row = pl.pallas_call(
        functools.partial(partial_kernel, noise_parts, jobs, known, scale),
        cost_estimate=pl.CostEstimate(flops=1, bytes_accessed=1, transcendentals=0),
        out_shape=[jax.ShapeDtypeStruct(o, jnp.float32) for o in [out] * 4 + squares],
        grid=(depth // block,),
        in_specs=[pl.BlockSpec(memory_space=pltpu.SMEM)]
        + [pl.BlockSpec(o.shape, lambda k: (0, 0)) for o in (old_n, old_x)]
        + [pl.BlockSpec((a.shape[0], block), lambda k: (0, k)) for a in (*flat, *datas)],
        out_specs=[pl.BlockSpec(out, lambda k: (0, 0, 0))] * 4
        + [pl.BlockSpec(o, lambda k: (0, 0)) for o in squares],
        scratch_shapes=[
            pltpu.VMEM((parts, share, total), jnp.float32),
            pltpu.VMEM((columns, LANES), jnp.float32),
        ],
        compiler_params=pltpu.CompilerParams(vmem_limit_bytes=48 * 2**20),
    )(where, old_n, old_x, *flat, *datas)
    return pieces, n_sq, x_row


def ring(x, shift):
    return lax.ppermute(x, "y", [(i, (i + shift) % 4) for i in range(4)])


def swap(x, axis):
    return lax.ppermute(x, axis, [(0, 1), (1, 0)])


SOURCES = [(0, 0, 0), (0, 0, 1), (0, 1, 0), (0, 1, 1), (-1, 0, 0), (-1, 0, 1), (1, 0, 0), (1, 0, 1)]
SOURCES += [(-1, 1, 0), (-1, 1, 1), (1, 1, 0), (1, 1, 1), (-2, 0, 0), (2, 0, 1), (-2, 1, 0), (2, 1, 1)]
ALONG_X = (0, 1, -1, 2)


def along_x(x, step):
    return lax.ppermute(x, "x", [(i, (i + step) % 4) for i in range(4)])


def tables(parts):
    zh, y, core = (lax.axis_index(a) for a in ("zh", "y", "core"))
    where, place = [], []
    for dz in range(2):
        for s, (dy, dc, half) in enumerate(SOURCES):
            inside = ((y + dy + 4) % 4 * 2 + (core + dc) % 2) * 2 + half
            where.append((zh + dz) % 2 * 16 + inside)
            place.append(16 + inside if dz else jnp.int32(s))
    x, zl = lax.axis_index("x"), lax.axis_index("zl")
    rows = [(zl + z) % 2 * 4 + (x + d + 4) % 4 for d in ALONG_X for z in range(2)]
    rows = jnp.pad(jnp.stack(rows), (0, len(where) - len(rows)))
    return jnp.stack([jnp.stack(where), jnp.stack(place), rows]).astype(jnp.int32)


def local(noise, data):
    temper = 0.5 / math.sqrt(F)
    scale = -1.0 / (F * temper)
    parts = 8
    half = noise.shape[0] // 2
    call = functools.partial(partial_call, scale, parts)
    where = tables(parts)
    here = jnp.stack([lax.axis_index("x"), lax.axis_index("zl")]).astype(jnp.int32)
    hold = lax.optimization_barrier

    u, w = ring(data, 1), ring(data, -1)
    far = swap(noise, "zh")
    data_c = swap(data, "core")
    u, w, far, data_c, data = hold((u, w, far, data_c, data))

    ua, wb = u[:half], w[half:]
    ua, wb, u, w, data = hold((ua, wb, u, w, data))
    u3, w3 = ring(ua, 1), ring(wb, -1)
    u_c, w_c = swap(u, "core"), swap(w, "core")
    other = swap(data, "zh")
    noises = [(noise,), (far,)]
    (a0, a1, a3, a2), n_sq, _ = call(here, noises, [data, data_c, u, w], (((0, 1), (0, 1, 2, 3)),))
    u_c, w_c, a0, a1, a2, a3 = hold((u_c, w_c, a0, a1, a2, a3))
    a1, a3 = along_x(a1, 1), along_x(a3, -1)
    (b0, b1, b3, b2), _, _ = call(here, noises, [u_c, w_c], (((0, 1), (0, 1)),), n_sq)
    a2 = along_x(a2, 2)
    b1, b3 = along_x(b1, 1), along_x(b3, -1)
    u3, w3, a1, a3, b0, b2 = hold((u3, w3, a1, a3, b0, b2))

    u3_c, w3_c = swap(u3, "core"), swap(w3, "core")
    (c0, c1, c3, c2), _, _ = call(here, noises, [u3, w3, u3_c, w3_c], (((0, 1), (0, 1, 2, 3)),), n_sq)
    b2 = along_x(b2, 2)
    c1, c3, c2 = along_x(c1, 1), along_x(c3, -1), along_x(c2, 2)
    b2, c1, c2, c3, other = hold((b2, c1, c2, c3, other))
    a, b, c = a0 + a1 + a2 + a3, b0 + b1 + b2 + b3, c0 + c1 + c2 + c3

    def halves(z):
        return jnp.stack([
            jnp.concatenate([p[z][:, i * n:(i + 1) * n] for p, n in ((a, 1024), (b, 512), (c, 512))], axis=1)
            for i in range(2)
        ])

    own = halves(0) + lax.ppermute(halves(1), "zl", [(0, 1), (1, 0)])
    own = jnp.stack([own[0], swap(own[1], "zh")])
    own, other = hold((own, other))
    others = lax.all_gather(other, ("y", "core"), axis=0, tiled=True)
    out = jax.ShapeDtypeStruct((2, SAMPLES), jnp.float32)

    steps = SAMP_STEPS + FEAT_STEPS
    once = lax.axis_index("x") // 8 + 1

    def spread(_, c):
        return column_update(row_call(sinkhorn_kernel, out, where, [own[None]], c), steps)

    c = lax.fori_loop(0, once, spread, jnp.zeros((1, SAMPLES), jnp.float32))
    shape = jax.ShapeDtypeStruct(own.shape, jnp.bfloat16)
    mine = row_call(exponentials_kernel, shape, where, [own[None]], c)
    both = jnp.stack([mine, lax.ppermute(mine, "zl", [(0, 1), (1, 0)])])
    mine, both = hold((mine, both))
    kernels = [both] + [along_x(both, -d) for d in ALONG_X[1:]]

    sums = jax.ShapeDtypeStruct((1, SAMPLES), jnp.float32)

    def balance(_, v):
        return 1.0 / column_sum(balance_call(balance_kernel, sums, where, [mine[None]], v), steps)

    v = lax.fori_loop(0, once, balance, jnp.ones((1, SAMPLES), jnp.float32))
    blocks = [data, data_c, u, w, u_c, w_c, u3, w3, u3_c, w3_c]
    for _ in range(2, ITERS):
        v = 1.0 / column_sum(balance_call(balance_kernel, sums, where, kernels, v), SAMP_STEPS)
    c = c + jnp.log(v)
    share = SAMPLES // parts
    start = (lax.axis_index("zl") * 4 + lax.axis_index("x")) * share
    column_out = lax.dynamic_slice_in_dim(c[0] * temper, start, share, 0)
    return (targets_call(where, kernels, v, [*blocks, others]), column_out)


def solution(mesh):
    fine = Mesh(mesh.devices.reshape(2, 4, 2, 2, 4), ("zh", "y", "core", "zl", "x"))
    samp, feat = ("zh", "y", "core"), FEAT
    in_specs = (P(samp, feat), P(samp, feat))
    out_specs = (P(samp, feat), P(feat))
    return jax.shard_map(local, mesh=fine, in_specs=in_specs, out_specs=out_specs, check_vma=False)
```

```python
import functools
import math

import jax
import jax.numpy as jnp
from jax import lax
from jax.experimental import pallas as pl
from jax.experimental.pallas import tpu as pltpu
from jax.sharding import Mesh, PartitionSpec as P

F = 32768
ITERS = 3
SAMPLES = 4096
LANES = 128
ROWS = 32
GROUP = 4
DEPTH = 2048
FEAT = ("zl", "x")


def tile_list(shapes):
    return [
        (k, g, n)
        for k, (_, groups, _, width) in enumerate(shapes)
        for g in range(groups)
        for n in range(0, width, LANES)
    ]


def row_pass(tiles, blocks, logits, where, c_ref, peak_ref, row_ref):
    def tile(f, t):
        k, g, n = tiles[t]
        return logits[k][f, g, :, n:n + LANES] + c_ref[:, lanes(where[0, t])]

    def maxima(f, _):
        acc = tile(f, 0)
        for t in range(1, len(tiles)):
            acc = jnp.maximum(acc, tile(f, t))
        peak_ref[pl.ds(f * ROWS, ROWS), :] = acc
        return 0

    lax.fori_loop(0, blocks, maxima, 0)
    peak = jnp.max(peak_ref[...], axis=1, keepdims=True)
    peak_ref[...] = jnp.broadcast_to(peak, peak_ref.shape)

    def totals(f, _):
        top = peak_ref[pl.ds(f * ROWS, ROWS), :]
        acc = jnp.exp(tile(f, 0) - top)
        for t in range(1, len(tiles)):
            acc = acc + jnp.exp(tile(f, t) - top)
        row_ref[pl.ds(f * ROWS, ROWS), :] = acc
        return 0

    lax.fori_loop(0, blocks, totals, 0)
    return jnp.sum(row_ref[...], axis=1, keepdims=True)


def lanes(tile):
    return pl.ds(pl.multiple_of(tile * LANES, LANES), LANES)


def sinkhorn_kernel(shapes, where, *refs):
    logits, (c_ref, out_ref, peak_ref, row_ref) = refs[:len(shapes)], refs[len(shapes):]
    tiles = tile_list(shapes)
    blocks = shapes[0][0]
    total = row_pass(tiles, blocks, logits, where, c_ref, peak_ref, row_ref)
    row_ref[...] = jnp.broadcast_to(-(peak_ref[:, 0:1] + jnp.log(total)), row_ref.shape)
    for first in range(0, len(tiles), GROUP):
        group = range(first, first + GROUP)

        def values(f, r, t):
            k, g, n = tiles[t]
            rows = row_ref[pl.ds(f * ROWS + r * 8, 8), :]
            return logits[k][f, g, r * 8:(r + 1) * 8, n:n + LANES] + rows

        def maxima(f, acc):
            for r in range(ROWS // 8):
                acc = [jnp.maximum(a, values(f, r, t)) for a, t in zip(acc, group)]
            return acc

        start = [jnp.full((8, LANES), -jnp.inf, jnp.float32) for _ in group]
        acc = lax.fori_loop(0, blocks, maxima, start)
        peaks = [jnp.max(a, axis=0, keepdims=True) for a in acc]

        def totals(f, acc):
            for r in range(ROWS // 8):
                acc = [a + jnp.exp(values(f, r, t) - p) for a, p, t in zip(acc, peaks, group)]
            return acc

        start = [jnp.zeros((8, LANES), jnp.float32) for _ in group]
        acc = lax.fori_loop(0, blocks, totals, start)
        for a, p, t in zip(acc, peaks, group):
            out_ref[0:1, lanes(where[0, t])] = p
            out_ref[1:2, lanes(where[0, t])] = jnp.sum(a, axis=0, keepdims=True)


def exponentials_kernel(shapes, where, *refs):
    logits, (c_ref, out_ref, peak_ref, _) = refs[:len(shapes)], refs[len(shapes):]
    tiles = tile_list(shapes[:1])
    for k, ref in enumerate(logits):
        acc = None
        for t, (_, g, n) in enumerate(tiles):
            x = ref[0, g, :, n:n + LANES] + c_ref[:, lanes(where[0, t])]
            acc = x if acc is None else jnp.maximum(acc, x)
        peak_ref[...] = jnp.broadcast_to(jnp.max(acc, axis=1, keepdims=True), peak_ref.shape)
        top = peak_ref[...]
        for t, (_, g, n) in enumerate(tiles):
            x = ref[0, g, :, n:n + LANES] + c_ref[:, lanes(where[0, t])]
            out_ref[k, g, :, n:n + LANES] = jnp.exp(x - top).astype(jnp.bfloat16)


def scaled_rows(tiles, kernels, where, v_ref, row_ref):
    for d, k_ref in enumerate(kernels):
        for z in range(k_ref.shape[0]):
            acc = None
            for t, (_, g, n) in enumerate(tiles):
                x = k_ref[z, g, :, n:n + LANES].astype(jnp.float32) * v_ref[:, lanes(where[0, t])]
                acc = x if acc is None else acc + x
            first = (d * k_ref.shape[0] + z) * ROWS
            row_ref[first:first + ROWS, :] = acc
    return jnp.sum(row_ref[...], axis=1, keepdims=True)


def balance_kernel(shapes, where, *refs):
    kernels, (v_ref, out_ref, row_ref) = refs[:len(shapes)], refs[len(shapes):]
    tiles = tile_list(((1,) + shapes[0][1:],))
    total = scaled_rows(tiles, kernels, where, v_ref, row_ref)
    row_ref[...] = jnp.broadcast_to(1.0 / total, row_ref.shape)
    for t, (_, g, n) in enumerate(tiles):
        acc = jnp.zeros((ROWS, LANES), jnp.float32)
        for d, k_ref in enumerate(kernels):
            for z in range(k_ref.shape[0]):
                first = (d * k_ref.shape[0] + z) * ROWS
                acc = acc + k_ref[z, g, :, n:n + LANES].astype(jnp.float32) * row_ref[first:first + ROWS, :]
        out_ref[0:1, lanes(where[0, t])] = jnp.sum(acc, axis=0, keepdims=True)


def targets_kernel(shapes, widths, where, *refs):
    n = len(shapes)
    kernels, v_ref, x_refs, (out_ref, row_ref, w_ref) = refs[:n], refs[n], refs[n + 1:-3], refs[-3:]

    @pl.when(pl.program_id(0) == 0)
    def _():
        tiles = tile_list(((1,) + shapes[0][1:],))
        total = scaled_rows(tiles, kernels, where, v_ref, row_ref)
        row_ref[...] = jnp.broadcast_to(1.0 / total, row_ref.shape)
        for d, k_ref in enumerate(kernels):
            for z in range(k_ref.shape[0]):
                first = (d * k_ref.shape[0] + z) * ROWS
                scale = row_ref[first:first + ROWS, :]
                rows = pl.ds(pl.multiple_of(where[2, d * k_ref.shape[0] + z] * ROWS, ROWS), ROWS)
                for t, (_, g, n) in enumerate(tiles):
                    x = k_ref[z, g, :, n:n + LANES].astype(jnp.float32) * v_ref[:, lanes(where[0, t])]
                    w_ref[rows, lanes(where[1, t])] = (x * scale).astype(jnp.bfloat16)

    first, acc = 0, None
    for x, width in zip(x_refs, widths):
        part = jnp.dot(w_ref[:, first:first + width], x[...], preferred_element_type=jnp.float32)
        acc = part if acc is None else acc + part
        first += width
    out_ref[...] = acc.astype(out_ref.dtype)


def targets_call(where, kernels, v, datas):
    shapes = tuple(a.shape for a in kernels)
    rows = sum(s[0] for s in shapes) * ROWS
    widths = tuple(d.shape[0] for d in datas)
    depth, block = datas[0].shape[1], 1024
    vmem = pl.BlockSpec(memory_space=pltpu.VMEM)
    return pl.pallas_call(
        functools.partial(targets_kernel, shapes, widths),
        out_shape=jax.ShapeDtypeStruct((rows, depth), jnp.bfloat16),
        grid=(depth // block,),
        in_specs=[pl.BlockSpec(memory_space=pltpu.SMEM)] + [vmem] * (len(kernels) + 1)
        + [pl.BlockSpec((w, block), lambda n: (0, n)) for w in widths],
        out_specs=pl.BlockSpec((rows, block), lambda n: (0, n)),
        scratch_shapes=[
            pltpu.VMEM((rows, LANES), jnp.float32),
            pltpu.VMEM((rows, sum(widths)), jnp.bfloat16),
        ],
        compiler_params=pltpu.CompilerParams(vmem_limit_bytes=48 * 2**20),
    )(where, *kernels, v, *datas)


def balance_call(kernel, out_shape, where, kernels, v):
    shapes = tuple(a.shape for a in kernels)
    rows = sum(s[0] for s in shapes) * ROWS
    vmem = pl.BlockSpec(memory_space=pltpu.VMEM)
    return pl.pallas_call(
        functools.partial(kernel, shapes),
        out_shape=out_shape,
        in_specs=[pl.BlockSpec(memory_space=pltpu.SMEM)] + [vmem] * (len(kernels) + 1),
        out_specs=vmem,
        scratch_shapes=[pltpu.VMEM((rows, LANES), jnp.float32)],
        compiler_params=pltpu.CompilerParams(vmem_limit_bytes=32 * 2**20),
    )(where, *kernels, v)


def row_call(kernel, out_shape, where, logits, c):
    shapes = tuple(a.shape for a in logits)
    rows = shapes[0][0] * ROWS
    vmem = pl.BlockSpec(memory_space=pltpu.VMEM)
    return pl.pallas_call(
        functools.partial(kernel, shapes),
        out_shape=out_shape,
        in_specs=[pl.BlockSpec(memory_space=pltpu.SMEM)] + [vmem] * (len(logits) + 1),
        out_specs=vmem,
        scratch_shapes=[pltpu.VMEM((rows, LANES), jnp.float32)] * 2,
        compiler_params=pltpu.CompilerParams(vmem_limit_bytes=32 * 2**20),
    )(where, *logits, c)


SAMP_RINGS = (("core", 2), ("y", 4), ("zh", 2))
ALL_RINGS = (("core", 2), ("y", 4), (("zh", "zl"), 4), ("x", 4))


def around(x, axis, n):
    def shift(k):
        return lax.ppermute(x, axis, [(i, (i + k) % n) for i in range(n)])

    if n == 2:
        return [(x, shift(1))]
    left, right, across = shift(1), shift(-1), shift(2)
    return [(x, across), (left, right)]


def combine(pairs):
    peak = functools.reduce(jnp.maximum, [p[0] for pair in pairs for p in pair])
    totals = [sum(p[1] * jnp.exp(p[0] - peak) for p in pair) for pair in pairs]
    return jnp.stack([peak, sum(totals)])


def column_sum(x, rings):
    for axis, n in rings:
        x = sum(a + b for a, b in around(x, axis, n))
    return x


def column_sum_in_pairs(x):
    steps = (("core", 2, 1), ("y", 4, 1), ("y", 4, 2), ("zh", 2, 1), ("zl", 2, 1), ("x", 4, 1), ("x", 4, 2))
    for axis, n, step in steps:
        x = x + lax.ppermute(x, axis, [(i, i ^ step) for i in range(n)])
    return x


def column_update(stats, rings):
    for axis, n in rings:
        stats = combine(around(stats, axis, n))
    return -(stats[0] + jnp.log(stats[1]))[None, :]


def lane_sums(x):
    acc = None
    for n in range(0, x.shape[1], LANES):
        v = x[:, n:n + LANES].astype(jnp.float32)
        acc = v * v if acc is None else acc + v * v
    return acc


def partial_kernel(noise_parts, jobs, known, scale, *refs):
    n_count = sum(noise_parts)
    x_count = 1 + max(x for _, xs in jobs for x in xs)
    where, old_n, old_x = refs[:3]
    n_refs, x_refs = refs[3:3 + n_count], refs[3 + n_count:3 + n_count + x_count]
    outs, (n_sq, x_row, acc, x_sq) = refs[3 + n_count + x_count:-4], refs[-4:]
    step = pl.program_id(0)
    parts, share, _ = acc.shape
    rows = parts * share
    starts = [sum(noise_parts[:q]) for q in range(len(noise_parts))]

    @pl.when(step == 0)
    def _():
        acc[...] = jnp.zeros_like(acc)
        n_sq[...] = jnp.zeros_like(n_sq)
        x_sq[...] = jnp.zeros_like(x_sq)

    places, first = [], 0
    for qs, xs in jobs:
        widths = [x_refs[x].shape[0] for x in xs]
        block = jnp.concatenate(
            [n_refs[starts[q] + p][...] for q in qs for p in range(noise_parts[q])], axis=0
        )
        others = jnp.concatenate([x_refs[x][...] for x in xs], axis=0)
        inner = lax.dot_general(
            block, others, (((1,), (1,)), ((), ())), preferred_element_type=jnp.float32
        )
        for i, q in enumerate(qs):
            at = first + i * sum(widths)
            part = inner[i * rows:(i + 1) * rows].reshape(parts, share, sum(widths))
            acc[:, :, at:at + sum(widths)] += part
            for x, width in zip(xs, widths):
                places.append((q, x, at))
                at += width
        first += len(qs) * sum(widths)
    x_starts = [sum(r.shape[0] for r in x_refs[:x]) for x in range(x_count)]
    for squares, blocks, seen in ((n_sq, n_refs, known[0]), (x_sq, x_refs, known[1])):
        start = 0
        for r in blocks:
            if start >= seen:
                squares[start:start + r.shape[0], :] += lane_sums(r[...])
            start += r.shape[0]

    @pl.when(step == pl.num_programs(0) - 1)
    def _():
        x_row[...] = lax.dot_general(
            jnp.ones((8, LANES), jnp.float32), x_sq[...], (((1,), (1,)), ((), ())),
            precision=lax.Precision.HIGHEST, preferred_element_type=jnp.float32,
        )[0:1]
        n_sq[...] = jnp.broadcast_to(jnp.sum(n_sq[...], axis=1, keepdims=True), n_sq.shape)
        if known[0]:
            n_sq[0:known[0], :] = old_n[...]
        if known[1]:
            x_row[:, 0:known[1]] = old_x[...]
        for d, out in zip((0, 1, -1, 2), outs):
            for z in range(2):
                f = (where[1] + z) % 2 * 4 + (where[0] + d + 4) % 4
                for q, x, at in places:
                    width = x_refs[x].shape[0]
                    own = n_sq[pl.ds(q * rows + f * share, share), 0:1]
                    other = x_row[:, x_starts[x]:x_starts[x] + width]
                    inner = acc[f, :, at:at + width]
                    out[z, :, at:at + width] = (own + other - 2.0 * inner) * scale


def partial_call(scale, parts, where, noises, datas, jobs, old_n=None, old_x=None):
    known = (0 if old_n is None else old_n.shape[0], 0 if old_x is None else old_x.shape[1])
    old_n = jnp.zeros((8, LANES), jnp.float32) if old_n is None else old_n
    old_x = jnp.zeros((1, LANES), jnp.float32) if old_x is None else old_x
    noise_parts = tuple(len(n) for n in noises)
    flat = [a for n in noises for a in n]
    rows, depth = sum(a.shape[0] for a in noises[0]), flat[0].shape[1]
    total = sum(len(qs) * sum(datas[x].shape[0] for x in xs) for qs, xs in jobs)
    share = rows // parts
    block = DEPTH
    out = (2, share, total)
    n_rows, columns = sum(a.shape[0] for a in flat), sum(d.shape[0] for d in datas)
    squares = [(n_rows, LANES), (1, columns)]
    *pieces, n_sq, x_row = pl.pallas_call(
        functools.partial(partial_kernel, noise_parts, jobs, known, scale),
        cost_estimate=pl.CostEstimate(flops=1, bytes_accessed=1, transcendentals=0),
        out_shape=[jax.ShapeDtypeStruct(o, jnp.float32) for o in [out] * 4 + squares],
        grid=(depth // block,),
        in_specs=[pl.BlockSpec(memory_space=pltpu.SMEM)]
        + [pl.BlockSpec(o.shape, lambda k: (0, 0)) for o in (old_n, old_x)]
        + [pl.BlockSpec((a.shape[0], block), lambda k: (0, k)) for a in (*flat, *datas)],
        out_specs=[pl.BlockSpec(out, lambda k: (0, 0, 0))] * 4
        + [pl.BlockSpec(o, lambda k: (0, 0)) for o in squares],
        scratch_shapes=[
            pltpu.VMEM((parts, share, total), jnp.float32),
            pltpu.VMEM((columns, LANES), jnp.float32),
        ],
        compiler_params=pltpu.CompilerParams(vmem_limit_bytes=48 * 2**20),
    )(where, old_n, old_x, *flat, *datas)
    return pieces, n_sq, x_row


def halves_kernel(u_ref, w_ref, a_ref, b_ref):
    a_ref[...] = u_ref[...]
    b_ref[...] = w_ref[...]


def halves_call(u, w):
    half, block = u.shape[0] // 2, 2048
    out = jax.ShapeDtypeStruct((half, u.shape[1]), u.dtype)
    return pl.pallas_call(
        halves_kernel,
        cost_estimate=pl.CostEstimate(flops=1, bytes_accessed=1, transcendentals=0),
        out_shape=[out, out],
        grid=(u.shape[1] // block,),
        in_specs=[pl.BlockSpec((half, block), lambda n: (0, n)), pl.BlockSpec((half, block), lambda n: (1, n))],
        out_specs=[pl.BlockSpec((half, block), lambda n: (0, n))] * 2,
    )(u, w)


def ring(x, shift):
    return lax.ppermute(x, "y", [(i, (i + shift) % 4) for i in range(4)])


def swap(x, axis):
    return lax.ppermute(x, axis, [(0, 1), (1, 0)])


SOURCES = [(0, 0, 0), (0, 0, 1), (0, 1, 0), (0, 1, 1), (-1, 0, 0), (-1, 0, 1), (1, 0, 0), (1, 0, 1)]
SOURCES += [(-1, 1, 0), (-1, 1, 1), (1, 1, 0), (1, 1, 1), (-2, 0, 0), (2, 0, 1), (-2, 1, 0), (2, 1, 1)]
ALONG_X = (0, 1, -1, 2)


def along_x(x, step):
    return lax.ppermute(x, "x", [(i, (i + step) % 4) for i in range(4)])


def tables(parts):
    zh, y, core = (lax.axis_index(a) for a in ("zh", "y", "core"))
    where, place = [], []
    for dz in range(2):
        for s, (dy, dc, half) in enumerate(SOURCES):
            inside = ((y + dy + 4) % 4 * 2 + (core + dc) % 2) * 2 + half
            where.append((zh + dz) % 2 * 16 + inside)
            place.append(16 + inside if dz else jnp.int32(s))
    x, zl = lax.axis_index("x"), lax.axis_index("zl")
    rows = [(zl + z) % 2 * 4 + (x + d + 4) % 4 for d in ALONG_X for z in range(2)]
    rows = jnp.pad(jnp.stack(rows), (0, len(where) - len(rows)))
    return jnp.stack([jnp.stack(where), jnp.stack(place), rows]).astype(jnp.int32)


def local(noise, data):
    temper = 0.5 / math.sqrt(F)
    scale = -1.0 / (F * temper)
    parts = 8
    half = noise.shape[0] // 2
    call = functools.partial(partial_call, scale, parts)
    where = tables(parts)
    here = jnp.stack([lax.axis_index("x"), lax.axis_index("zl")]).astype(jnp.int32)
    hold = lax.optimization_barrier

    u, w = ring(data, 1), ring(data, -1)
    far = swap(noise, "zh")
    data_c = swap(data, "core")
    (k0, k1, k3, k2), n_sq, x_row = call(here, [(noise,)], [data, data_c], (((0,), (0, 1)),))
    k1, k3, k2 = along_x(k1, 1), along_x(k3, -1), along_x(k2, 2)
    u, w, far, data_c, data, k0, k1, k2, k3 = hold((u, w, far, data_c, data, k0, k1, k2, k3))

    ua, wb = halves_call(u, w)
    ua, wb, u, w, data = hold((ua, wb, u, w, data))
    u3, w3 = ring(ua, 1), ring(wb, -1)
    u_c, w_c = swap(u, "core"), swap(w, "core")
    other = swap(data, "zh")
    noises = [(noise,), (far,)]
    jobs = (((0, 1), (2, 3)), ((1,), (0, 1)))
    (a0, a1, a3, a2), n_sq, _ = call(here, noises, [data, data_c, u, w], jobs, n_sq, x_row)
    u_c, w_c, a0, a1, a2, a3 = hold((u_c, w_c, a0, a1, a2, a3))
    a1, a3 = along_x(a1, 1), along_x(a3, -1)
    (b0, b1, b3, b2), _, _ = call(here, noises, [u_c, w_c], (((0, 1), (0, 1)),), n_sq)
    a2 = along_x(a2, 2)
    b1, b3 = along_x(b1, 1), along_x(b3, -1)
    u3, w3, a1, a3, b0, b2 = hold((u3, w3, a1, a3, b0, b2))

    u3_c, w3_c = swap(u3, "core"), swap(w3, "core")
    (c0, c1, c3, c2), _, _ = call(here, noises, [u3, w3, u3_c, w3_c], (((0, 1), (0, 1, 2, 3)),), n_sq)
    b2 = along_x(b2, 2)
    c1, c3, c2 = along_x(c1, 1), along_x(c3, -1), along_x(c2, 2)
    k, a = k0 + k1 + k2 + k3, a0 + a1 + a2 + a3

    def early(z):
        return jnp.stack([
            jnp.concatenate([k[z], a[z][:, :512]], axis=1),
            jnp.concatenate([a[z][:, 1024:], a[z][:, 512:1024]], axis=1),
        ])

    b2, c1, c2, c3, other = hold((b2, c1, c2, c3, other))
    b, c = b0 + b1 + b2 + b3, c0 + c1 + c2 + c3

    def late(z):
        return jnp.stack([
            jnp.concatenate([p[z][:, i * 512:(i + 1) * 512] for p in (b, c)], axis=1) for i in range(2)
        ])

    def across_z(x, step):
        return lax.ppermute(x, ("zh", "zl"), [(i, i ^ step) for i in range(4)])

    mine, theirs = (jnp.concatenate([early(z), late(z)], axis=2) for z in range(2))
    own = jnp.stack([
        mine[0] + across_z(theirs[0], 1), across_z(mine[1], 2) + across_z(theirs[1], 3)
    ])
    own, other = hold((own, other))
    others = lax.all_gather(other, ("y", "core"), axis=0, tiled=True)
    out = jax.ShapeDtypeStruct((2, SAMPLES), jnp.float32)

    once = lax.axis_index("x") // 8 + 1

    def spread(_, c):
        return column_update(row_call(sinkhorn_kernel, out, where, [own[None]], c), ALL_RINGS)

    pair = lax.ppermute(own, "zl", [(0, 1), (1, 0)])
    c = lax.fori_loop(0, once, spread, jnp.zeros((1, SAMPLES), jnp.float32))
    c, pair = hold((c, pair))
    shape = jax.ShapeDtypeStruct((2,) + own.shape, jnp.bfloat16)
    both = row_call(exponentials_kernel, shape, where, [own[None], pair[None]], c)
    kernels = [both] + [along_x(both, -d) for d in ALONG_X[1:]]

    sums = jax.ShapeDtypeStruct((1, SAMPLES), jnp.float32)

    def balance(_, v):
        return 1.0 / column_sum_in_pairs(balance_call(balance_kernel, sums, where, [both[:1]], v))

    v = lax.fori_loop(0, once, balance, jnp.ones((1, SAMPLES), jnp.float32))
    blocks = [data, data_c, u, w, u_c, w_c, u3, w3, u3_c, w3_c]
    for _ in range(2, ITERS):
        v = 1.0 / column_sum(balance_call(balance_kernel, sums, where, kernels, v), SAMP_RINGS)
    c = c + jnp.log(v)
    share = SAMPLES // parts
    start = (lax.axis_index("zl") * 4 + lax.axis_index("x")) * share
    column_out = lax.dynamic_slice_in_dim(c[0] * temper, start, share, 0)
    return (targets_call(where, kernels, v, [*blocks, others]), column_out)


def solution(mesh):
    fine = Mesh(mesh.devices.reshape(2, 4, 2, 2, 4), ("zh", "y", "core", "zl", "x"))
    samp, feat = ("zh", "y", "core"), FEAT
    in_specs = (P(samp, feat), P(samp, feat))
    out_specs = (P(samp, feat), P(feat))
    return jax.shard_map(local, mesh=fine, in_specs=in_specs, out_specs=out_specs, check_vma=False)
```

```python
import functools
import math

import jax
import jax.numpy as jnp
from jax import lax
from jax.experimental import pallas as pl
from jax.experimental.pallas import tpu as pltpu
from jax.sharding import Mesh, PartitionSpec as P

F = 32768
ITERS = 3
SAMPLES = 4096
LANES = 128
ROWS = 32
GROUP = 4
DEPTH = 2048
FEAT = ("zl", "x")


def tile_list(shapes):
    return [
        (k, g, n)
        for k, (_, groups, _, width) in enumerate(shapes)
        for g in range(groups)
        for n in range(0, width, LANES)
    ]


def row_pass(tiles, blocks, logits, where, c_ref, peak_ref, row_ref):
    def tile(f, t):
        k, g, n = tiles[t]
        return logits[k][f, g, :, n:n + LANES] + c_ref[:, lanes(where[0, t])]

    def maxima(f, _):
        acc = tile(f, 0)
        for t in range(1, len(tiles)):
            acc = jnp.maximum(acc, tile(f, t))
        peak_ref[pl.ds(f * ROWS, ROWS), :] = acc
        return 0

    lax.fori_loop(0, blocks, maxima, 0)
    peak = jnp.max(peak_ref[...], axis=1, keepdims=True)
    peak_ref[...] = jnp.broadcast_to(peak, peak_ref.shape)

    def totals(f, _):
        top = peak_ref[pl.ds(f * ROWS, ROWS), :]
        acc = jnp.exp(tile(f, 0) - top)
        for t in range(1, len(tiles)):
            acc = acc + jnp.exp(tile(f, t) - top)
        row_ref[pl.ds(f * ROWS, ROWS), :] = acc
        return 0

    lax.fori_loop(0, blocks, totals, 0)
    return jnp.sum(row_ref[...], axis=1, keepdims=True)


def lanes(tile):
    return pl.ds(pl.multiple_of(tile * LANES, LANES), LANES)


def sinkhorn_kernel(shapes, where, *refs):
    logits, (c_ref, out_ref, peak_ref, row_ref) = refs[:len(shapes)], refs[len(shapes):]
    tiles = tile_list(shapes)
    blocks = shapes[0][0]
    total = row_pass(tiles, blocks, logits, where, c_ref, peak_ref, row_ref)
    row_ref[...] = jnp.broadcast_to(-(peak_ref[:, 0:1] + jnp.log(total)), row_ref.shape)
    for first in range(0, len(tiles), GROUP):
        group = range(first, first + GROUP)

        def values(f, r, t):
            k, g, n = tiles[t]
            rows = row_ref[pl.ds(f * ROWS + r * 8, 8), :]
            return logits[k][f, g, r * 8:(r + 1) * 8, n:n + LANES] + rows

        def maxima(f, acc):
            for r in range(ROWS // 8):
                acc = [jnp.maximum(a, values(f, r, t)) for a, t in zip(acc, group)]
            return acc

        start = [jnp.full((8, LANES), -jnp.inf, jnp.float32) for _ in group]
        acc = lax.fori_loop(0, blocks, maxima, start)
        peaks = [jnp.max(a, axis=0, keepdims=True) for a in acc]

        def totals(f, acc):
            for r in range(ROWS // 8):
                acc = [a + jnp.exp(values(f, r, t) - p) for a, p, t in zip(acc, peaks, group)]
            return acc

        start = [jnp.zeros((8, LANES), jnp.float32) for _ in group]
        acc = lax.fori_loop(0, blocks, totals, start)
        for a, p, t in zip(acc, peaks, group):
            out_ref[0:1, lanes(where[0, t])] = p
            out_ref[1:2, lanes(where[0, t])] = jnp.sum(a, axis=0, keepdims=True)


def exponentials_kernel(shapes, where, *refs):
    logits, (c_ref, out_ref, peak_ref, _) = refs[:len(shapes)], refs[len(shapes):]
    tiles = tile_list(shapes[:1])
    for k, ref in enumerate(logits):
        acc = None
        for t, (_, g, n) in enumerate(tiles):
            x = ref[0, g, :, n:n + LANES] + c_ref[:, lanes(where[0, t])]
            acc = x if acc is None else jnp.maximum(acc, x)
        peak_ref[...] = jnp.broadcast_to(jnp.max(acc, axis=1, keepdims=True), peak_ref.shape)
        top = peak_ref[...]
        for t, (_, g, n) in enumerate(tiles):
            x = ref[0, g, :, n:n + LANES] + c_ref[:, lanes(where[0, t])]
            out_ref[k, g, :, n:n + LANES] = jnp.exp(x - top).astype(jnp.bfloat16)


def scaled_rows(tiles, kernels, where, v_ref, row_ref):
    for d, k_ref in enumerate(kernels):
        for z in range(k_ref.shape[0]):
            acc = None
            for t, (_, g, n) in enumerate(tiles):
                x = k_ref[z, g, :, n:n + LANES].astype(jnp.float32) * v_ref[:, lanes(where[0, t])]
                acc = x if acc is None else acc + x
            first = (d * k_ref.shape[0] + z) * ROWS
            row_ref[first:first + ROWS, :] = acc
    return jnp.sum(row_ref[...], axis=1, keepdims=True)


def balance_kernel(shapes, where, *refs):
    kernels, (v_ref, out_ref, row_ref) = refs[:len(shapes)], refs[len(shapes):]
    tiles = tile_list(((1,) + shapes[0][1:],))
    total = scaled_rows(tiles, kernels, where, v_ref, row_ref)
    row_ref[...] = jnp.broadcast_to(1.0 / total, row_ref.shape)
    for t, (_, g, n) in enumerate(tiles):
        acc = jnp.zeros((ROWS, LANES), jnp.float32)
        for d, k_ref in enumerate(kernels):
            for z in range(k_ref.shape[0]):
                first = (d * k_ref.shape[0] + z) * ROWS
                acc = acc + k_ref[z, g, :, n:n + LANES].astype(jnp.float32) * row_ref[first:first + ROWS, :]
        out_ref[0:1, lanes(where[0, t])] = jnp.sum(acc, axis=0, keepdims=True)


def targets_kernel(shapes, widths, where, *refs):
    n = len(shapes)
    kernels, v_ref, x_refs, (out_ref, row_ref, w_ref) = refs[:n], refs[n], refs[n + 1:-3], refs[-3:]

    @pl.when(pl.program_id(0) == 0)
    def _():
        tiles = tile_list(((1,) + shapes[0][1:],))
        total = scaled_rows(tiles, kernels, where, v_ref, row_ref)
        row_ref[...] = jnp.broadcast_to(1.0 / total, row_ref.shape)
        for d, k_ref in enumerate(kernels):
            for z in range(k_ref.shape[0]):
                first = (d * k_ref.shape[0] + z) * ROWS
                scale = row_ref[first:first + ROWS, :]
                rows = pl.ds(pl.multiple_of(where[2, d * k_ref.shape[0] + z] * ROWS, ROWS), ROWS)
                for t, (_, g, n) in enumerate(tiles):
                    x = k_ref[z, g, :, n:n + LANES].astype(jnp.float32) * v_ref[:, lanes(where[0, t])]
                    w_ref[rows, lanes(where[1, t])] = (x * scale).astype(jnp.bfloat16)

    most = jnp.concatenate([x[...] for x in x_refs[:-1]], axis=0)
    first = sum(widths[:-1])
    acc = jnp.dot(w_ref[:, :first], most, preferred_element_type=jnp.float32)
    acc += jnp.dot(w_ref[:, first:], x_refs[-1][...], preferred_element_type=jnp.float32)
    out_ref[...] = acc.astype(out_ref.dtype)


def targets_call(where, kernels, v, datas):
    shapes = tuple(a.shape for a in kernels)
    rows = sum(s[0] for s in shapes) * ROWS
    widths = tuple(d.shape[0] for d in datas)
    depth, block = datas[0].shape[1], 1024
    vmem = pl.BlockSpec(memory_space=pltpu.VMEM)
    return pl.pallas_call(
        functools.partial(targets_kernel, shapes, widths),
        out_shape=jax.ShapeDtypeStruct((rows, depth), jnp.bfloat16),
        grid=(depth // block,),
        in_specs=[pl.BlockSpec(memory_space=pltpu.SMEM)] + [vmem] * (len(kernels) + 1)
        + [pl.BlockSpec((w, block), lambda n: (0, n)) for w in widths],
        out_specs=pl.BlockSpec((rows, block), lambda n: (0, n)),
        scratch_shapes=[
            pltpu.VMEM((rows, LANES), jnp.float32),
            pltpu.VMEM((rows, sum(widths)), jnp.bfloat16),
        ],
        compiler_params=pltpu.CompilerParams(vmem_limit_bytes=48 * 2**20),
    )(where, *kernels, v, *datas)


def balance_call(kernel, out_shape, where, kernels, v):
    shapes = tuple(a.shape for a in kernels)
    rows = sum(s[0] for s in shapes) * ROWS
    vmem = pl.BlockSpec(memory_space=pltpu.VMEM)
    return pl.pallas_call(
        functools.partial(kernel, shapes),
        out_shape=out_shape,
        in_specs=[pl.BlockSpec(memory_space=pltpu.SMEM)] + [vmem] * (len(kernels) + 1),
        out_specs=vmem,
        scratch_shapes=[pltpu.VMEM((rows, LANES), jnp.float32)],
        compiler_params=pltpu.CompilerParams(vmem_limit_bytes=32 * 2**20),
    )(where, *kernels, v)


def row_call(kernel, out_shape, where, logits, c):
    shapes = tuple(a.shape for a in logits)
    rows = shapes[0][0] * ROWS
    vmem = pl.BlockSpec(memory_space=pltpu.VMEM)
    return pl.pallas_call(
        functools.partial(kernel, shapes),
        out_shape=out_shape,
        in_specs=[pl.BlockSpec(memory_space=pltpu.SMEM)] + [vmem] * (len(logits) + 1),
        out_specs=vmem,
        scratch_shapes=[pltpu.VMEM((rows, LANES), jnp.float32)] * 2,
        compiler_params=pltpu.CompilerParams(vmem_limit_bytes=32 * 2**20),
    )(where, *logits, c)


SAMP_RINGS = (("core", 2), ("y", 4), ("zh", 2))
ALL_RINGS = (("core", 2), ("y", 4), (("zh", "zl"), 4), ("x", 4))


def around(x, axis, n):
    def shift(k):
        return lax.ppermute(x, axis, [(i, (i + k) % n) for i in range(n)])

    if n == 2:
        return [(x, shift(1))]
    left, right, across = shift(1), shift(-1), shift(2)
    return [(x, across), (left, right)]


def combine(pairs):
    peak = functools.reduce(jnp.maximum, [p[0] for pair in pairs for p in pair])
    totals = [sum(p[1] * jnp.exp(p[0] - peak) for p in pair) for pair in pairs]
    return jnp.stack([peak, sum(totals)])


def column_sum(x, rings):
    for axis, n in rings:
        x = sum(a + b for a, b in around(x, axis, n))
    return x


def column_sum_in_pairs(x):
    steps = (("core", 2, 1), ("y", 4, 1), ("y", 4, 2), ("zh", 2, 1), ("x", 4, 1), ("x", 4, 2))
    for axis, n, step in steps:
        x = x + lax.ppermute(x, axis, [(i, i ^ step) for i in range(n)])
    return x


def column_update(stats, rings):
    for axis, n in rings:
        stats = combine(around(stats, axis, n))
    return -(stats[0] + jnp.log(stats[1]))[None, :]


def lane_sums(x):
    acc = None
    for n in range(0, x.shape[1], LANES):
        v = x[:, n:n + LANES].astype(jnp.float32)
        acc = v * v if acc is None else acc + v * v
    return acc


def partial_kernel(noise_parts, jobs, known, scale, *refs):
    n_count = sum(noise_parts)
    x_count = 1 + max(x for _, xs in jobs for x in xs)
    where, old_n, old_x = refs[:3]
    n_refs, x_refs = refs[3:3 + n_count], refs[3 + n_count:3 + n_count + x_count]
    outs, (n_sq, x_row, acc, x_sq) = refs[3 + n_count + x_count:-4], refs[-4:]
    step = pl.program_id(0)
    parts, share, _ = acc.shape
    rows = parts * share
    starts = [sum(noise_parts[:q]) for q in range(len(noise_parts))]

    @pl.when(step == 0)
    def _():
        acc[...] = jnp.zeros_like(acc)
        n_sq[...] = jnp.zeros_like(n_sq)
        x_sq[...] = jnp.zeros_like(x_sq)

    places, first = [], 0
    for qs, xs in jobs:
        widths = [x_refs[x].shape[0] for x in xs]
        block = jnp.concatenate(
            [n_refs[starts[q] + p][...] for q in qs for p in range(noise_parts[q])], axis=0
        )
        others = jnp.concatenate([x_refs[x][...] for x in xs], axis=0)
        inner = lax.dot_general(
            block, others, (((1,), (1,)), ((), ())), preferred_element_type=jnp.float32
        )
        for i, q in enumerate(qs):
            at = first + i * sum(widths)
            part = inner[i * rows:(i + 1) * rows].reshape(parts, share, sum(widths))
            acc[:, :, at:at + sum(widths)] += part
            for x, width in zip(xs, widths):
                places.append((q, x, at))
                at += width
        first += len(qs) * sum(widths)
    x_starts = [sum(r.shape[0] for r in x_refs[:x]) for x in range(x_count)]
    for squares, blocks, seen in ((n_sq, n_refs, known[0]), (x_sq, x_refs, known[1])):
        start = 0
        for r in blocks:
            if start >= seen:
                squares[start:start + r.shape[0], :] += lane_sums(r[...])
            start += r.shape[0]

    @pl.when(step == pl.num_programs(0) - 1)
    def _():
        x_row[...] = lax.dot_general(
            jnp.ones((8, LANES), jnp.float32), x_sq[...], (((1,), (1,)), ((), ())),
            precision=lax.Precision.HIGHEST, preferred_element_type=jnp.float32,
        )[0:1]
        n_sq[...] = jnp.broadcast_to(jnp.sum(n_sq[...], axis=1, keepdims=True), n_sq.shape)
        if known[0]:
            n_sq[0:known[0], :] = old_n[...]
        if known[1]:
            x_row[:, 0:known[1]] = old_x[...]
        for d, out in zip((0, 1, -1, 2), outs):
            for z in range(2):
                f = (where[1] + z) % 2 * 4 + (where[0] + d + 4) % 4
                for q, x, at in places:
                    width = x_refs[x].shape[0]
                    own = n_sq[pl.ds(q * rows + f * share, share), 0:1]
                    other = x_row[:, x_starts[x]:x_starts[x] + width]
                    inner = acc[f, :, at:at + width]
                    out[z, :, at:at + width] = (own + other - 2.0 * inner) * scale


def partial_call(scale, parts, where, noises, datas, jobs, old_n=None, old_x=None):
    known = (0 if old_n is None else old_n.shape[0], 0 if old_x is None else old_x.shape[1])
    old_n = jnp.zeros((8, LANES), jnp.float32) if old_n is None else old_n
    old_x = jnp.zeros((1, LANES), jnp.float32) if old_x is None else old_x
    noise_parts = tuple(len(n) for n in noises)
    flat = [a for n in noises for a in n]
    rows, depth = sum(a.shape[0] for a in noises[0]), flat[0].shape[1]
    total = sum(len(qs) * sum(datas[x].shape[0] for x in xs) for qs, xs in jobs)
    share = rows // parts
    block = DEPTH
    out = (2, share, total)
    n_rows, columns = sum(a.shape[0] for a in flat), sum(d.shape[0] for d in datas)
    squares = [(n_rows, LANES), (1, columns)]
    *pieces, n_sq, x_row = pl.pallas_call(
        functools.partial(partial_kernel, noise_parts, jobs, known, scale),
        cost_estimate=pl.CostEstimate(flops=1, bytes_accessed=1, transcendentals=0),
        out_shape=[jax.ShapeDtypeStruct(o, jnp.float32) for o in [out] * 4 + squares],
        grid=(depth // block,),
        in_specs=[pl.BlockSpec(memory_space=pltpu.SMEM)]
        + [pl.BlockSpec(o.shape, lambda k: (0, 0)) for o in (old_n, old_x)]
        + [pl.BlockSpec((a.shape[0], block), lambda k: (0, k)) for a in (*flat, *datas)],
        out_specs=[pl.BlockSpec(out, lambda k: (0, 0, 0))] * 4
        + [pl.BlockSpec(o, lambda k: (0, 0)) for o in squares],
        scratch_shapes=[
            pltpu.VMEM((parts, share, total), jnp.float32),
            pltpu.VMEM((columns, LANES), jnp.float32),
        ],
        compiler_params=pltpu.CompilerParams(vmem_limit_bytes=48 * 2**20),
    )(where, old_n, old_x, *flat, *datas)
    return pieces, n_sq, x_row


def halves_kernel(u_ref, w_ref, a_ref, b_ref):
    a_ref[...] = u_ref[...]
    b_ref[...] = w_ref[...]


def halves_call(u, w):
    half, block = u.shape[0] // 2, 2048
    out = jax.ShapeDtypeStruct((half, u.shape[1]), u.dtype)
    return pl.pallas_call(
        halves_kernel,
        cost_estimate=pl.CostEstimate(flops=1, bytes_accessed=1, transcendentals=0),
        out_shape=[out, out],
        grid=(u.shape[1] // block,),
        in_specs=[pl.BlockSpec((half, block), lambda n: (0, n)), pl.BlockSpec((half, block), lambda n: (1, n))],
        out_specs=[pl.BlockSpec((half, block), lambda n: (0, n))] * 2,
    )(u, w)


def ring(x, shift):
    return lax.ppermute(x, "y", [(i, (i + shift) % 4) for i in range(4)])


def swap(x, axis):
    return lax.ppermute(x, axis, [(0, 1), (1, 0)])


SOURCES = [(0, 0, 0), (0, 0, 1), (0, 1, 0), (0, 1, 1), (-1, 0, 0), (-1, 0, 1), (1, 0, 0), (1, 0, 1)]
SOURCES += [(-1, 1, 0), (-1, 1, 1), (1, 1, 0), (1, 1, 1), (-2, 0, 0), (2, 0, 1), (-2, 1, 0), (2, 1, 1)]
ALONG_X = (0, 1, -1, 2)


def along_x(x, step):
    return lax.ppermute(x, "x", [(i, (i + step) % 4) for i in range(4)])


def tables(parts):
    zh, y, core = (lax.axis_index(a) for a in ("zh", "y", "core"))
    where, place = [], []
    for dz in range(2):
        for s, (dy, dc, half) in enumerate(SOURCES):
            inside = ((y + dy + 4) % 4 * 2 + (core + dc) % 2) * 2 + half
            where.append((zh + dz) % 2 * 16 + inside)
            place.append(16 + inside if dz else jnp.int32(s))
    x, zl = lax.axis_index("x"), lax.axis_index("zl")
    rows = [(zl + z) % 2 * 4 + (x + d + 4) % 4 for d in ALONG_X for z in range(2)]
    rows = jnp.pad(jnp.stack(rows), (0, len(where) - len(rows)))
    return jnp.stack([jnp.stack(where), jnp.stack(place), rows]).astype(jnp.int32)


def local(noise, data):
    temper = 0.5 / math.sqrt(F)
    scale = -1.0 / (F * temper)
    parts = 8
    half = noise.shape[0] // 2
    call = functools.partial(partial_call, scale, parts)
    where = tables(parts)
    here = jnp.stack([lax.axis_index("x"), lax.axis_index("zl")]).astype(jnp.int32)
    hold = lax.optimization_barrier

    u, w = ring(data, 1), ring(data, -1)
    far = swap(noise, "zh")
    data_c = swap(data, "core")
    (k0, k1, k3, k2), n_sq, x_row = call(here, [(noise,)], [data, data_c], (((0,), (0, 1)),))
    k1, k3, k2 = along_x(k1, 1), along_x(k3, -1), along_x(k2, 2)
    u, w, far, data_c, data, k0, k1, k2, k3 = hold((u, w, far, data_c, data, k0, k1, k2, k3))

    ua, wb = halves_call(u, w)
    ua, wb, u, w, data = hold((ua, wb, u, w, data))
    u3, w3 = ring(ua, 1), ring(wb, -1)
    u_c, w_c = swap(u, "core"), swap(w, "core")
    other = swap(data, "zh")
    noises = [(noise,), (far,)]
    jobs = (((0, 1), (2, 3)), ((1,), (0, 1)))
    (a0, a1, a3, a2), n_sq, _ = call(here, noises, [data, data_c, u, w], jobs, n_sq, x_row)
    u_c, w_c, a0, a1, a2, a3 = hold((u_c, w_c, a0, a1, a2, a3))
    a1, a3 = along_x(a1, 1), along_x(a3, -1)
    (b0, b1, b3, b2), _, _ = call(here, noises, [u_c, w_c], (((0, 1), (0, 1)),), n_sq)
    a2 = along_x(a2, 2)
    b1, b3 = along_x(b1, 1), along_x(b3, -1)
    u3, w3, a1, a3, b0, b2 = hold((u3, w3, a1, a3, b0, b2))

    u3_c, w3_c = swap(u3, "core"), swap(w3, "core")
    (c0, c1, c3, c2), _, _ = call(here, noises, [u3, w3, u3_c, w3_c], (((0, 1), (0, 1, 2, 3)),), n_sq)
    b2 = along_x(b2, 2)
    c1, c3, c2 = along_x(c1, 1), along_x(c3, -1), along_x(c2, 2)
    k, a = k0 + k1 + k2 + k3, a0 + a1 + a2 + a3

    def early(z):
        return jnp.stack([
            jnp.concatenate([k[z], a[z][:, :512]], axis=1),
            jnp.concatenate([a[z][:, 1024:], a[z][:, 512:1024]], axis=1),
        ])

    b2, c1, c2, c3, other = hold((b2, c1, c2, c3, other))
    b, c = b0 + b1 + b2 + b3, c0 + c1 + c2 + c3

    def late(z):
        return jnp.stack([
            jnp.concatenate([p[z][:, i * 512:(i + 1) * 512] for p in (b, c)], axis=1) for i in range(2)
        ])

    def across_z(x, step):
        return lax.ppermute(x, ("zh", "zl"), [(i, i ^ step) for i in range(4)])

    mine, theirs = (jnp.concatenate([early(z), late(z)], axis=2) for z in range(2))
    mine, theirs, other = hold((mine, theirs, other))
    others = lax.all_gather(other, ("y", "core"), axis=0, tiled=True)
    out = jax.ShapeDtypeStruct((2, SAMPLES), jnp.float32)

    once = lax.axis_index("x") // 8 + 1

    once = lax.axis_index("x") // 8 + 1

    def to_owners(_, acc):
        return acc + jnp.stack([
            mine[0] + across_z(theirs[0], 1), across_z(mine[1], 2) + across_z(theirs[1], 3)
        ])

    def spread(_, c):
        return column_update(row_call(sinkhorn_kernel, out, where, [own[None]], c), ALL_RINGS)

    own = lax.fori_loop(0, once, to_owners, jnp.zeros(mine.shape, jnp.float32))
    pair = lax.ppermute(own, "zl", [(0, 1), (1, 0)])
    c = lax.fori_loop(0, once, spread, jnp.zeros((1, SAMPLES), jnp.float32))
    c, pair = hold((c, pair))
    shape = jax.ShapeDtypeStruct((2,) + own.shape, jnp.bfloat16)
    both = row_call(exponentials_kernel, shape, where, [own[None], pair[None]], c)
    kernels = [both] + [along_x(both, -d) for d in ALONG_X[1:]]

    sums = jax.ShapeDtypeStruct((1, SAMPLES), jnp.float32)

    def balance(_, v):
        return 1.0 / column_sum_in_pairs(balance_call(balance_kernel, sums, where, [both], v))

    v = lax.fori_loop(0, once, balance, jnp.ones((1, SAMPLES), jnp.float32))
    blocks = [data, data_c, u, w, u_c, w_c, u3, w3, u3_c, w3_c]
    for _ in range(2, ITERS):
        v = 1.0 / column_sum(balance_call(balance_kernel, sums, where, kernels, v), SAMP_RINGS)
    c = c + jnp.log(v)
    share = SAMPLES // parts
    start = (lax.axis_index("zl") * 4 + lax.axis_index("x")) * share
    column_out = lax.dynamic_slice_in_dim(c[0] * temper, start, share, 0)
    return (targets_call(where, kernels, v, [*blocks, others]), column_out)


def solution(mesh):
    fine = Mesh(mesh.devices.reshape(2, 4, 2, 2, 4), ("zh", "y", "core", "zl", "x"))
    samp, feat = ("zh", "y", "core"), FEAT
    in_specs = (P(samp, feat), P(samp, feat))
    out_specs = (P(samp, feat), P(feat))
    return jax.shard_map(local, mesh=fine, in_specs=in_specs, out_specs=out_specs, check_vma=False)
```

```python
import functools
import math

import jax
import jax.numpy as jnp
from jax import lax
from jax.experimental import pallas as pl
from jax.experimental.pallas import tpu as pltpu
from jax.sharding import Mesh, PartitionSpec as P

F = 32768
ITERS = 3
SAMPLES = 4096
LANES = 128
ROWS = 32
GROUP = 4
DEPTH = 2048
FEAT = ("zl", "x")


def tile_list(shapes):
    return [
        (k, g, n)
        for k, (_, groups, _, width) in enumerate(shapes)
        for g in range(groups)
        for n in range(0, width, LANES)
    ]


def row_pass(tiles, blocks, logits, where, c_ref, peak_ref, row_ref):
    def tile(f, t):
        k, g, n = tiles[t]
        return logits[k][f, g, :, n:n + LANES] + c_ref[:, lanes(where[0, t])]

    def maxima(f, _):
        acc = tile(f, 0)
        for t in range(1, len(tiles)):
            acc = jnp.maximum(acc, tile(f, t))
        peak_ref[pl.ds(f * ROWS, ROWS), :] = acc
        return 0

    lax.fori_loop(0, blocks, maxima, 0)
    peak = jnp.max(peak_ref[...], axis=1, keepdims=True)
    peak_ref[...] = jnp.broadcast_to(peak, peak_ref.shape)

    def totals(f, _):
        top = peak_ref[pl.ds(f * ROWS, ROWS), :]
        acc = jnp.exp(tile(f, 0) - top)
        for t in range(1, len(tiles)):
            acc = acc + jnp.exp(tile(f, t) - top)
        row_ref[pl.ds(f * ROWS, ROWS), :] = acc
        return 0

    lax.fori_loop(0, blocks, totals, 0)
    return jnp.sum(row_ref[...], axis=1, keepdims=True)


def lanes(tile):
    return pl.ds(pl.multiple_of(tile * LANES, LANES), LANES)


def sinkhorn_kernel(shapes, where, *refs):
    logits, (c_ref, out_ref, peak_ref, row_ref) = refs[:len(shapes)], refs[len(shapes):]
    tiles = tile_list(shapes)
    blocks = shapes[0][0]
    total = row_pass(tiles, blocks, logits, where, c_ref, peak_ref, row_ref)
    row_ref[...] = jnp.broadcast_to(-(peak_ref[:, 0:1] + jnp.log(total)), row_ref.shape)
    for first in range(0, len(tiles), GROUP):
        group = range(first, first + GROUP)

        def values(f, r, t):
            k, g, n = tiles[t]
            rows = row_ref[pl.ds(f * ROWS + r * 8, 8), :]
            return logits[k][f, g, r * 8:(r + 1) * 8, n:n + LANES] + rows

        def maxima(f, acc):
            for r in range(ROWS // 8):
                acc = [jnp.maximum(a, values(f, r, t)) for a, t in zip(acc, group)]
            return acc

        start = [jnp.full((8, LANES), -jnp.inf, jnp.float32) for _ in group]
        acc = lax.fori_loop(0, blocks, maxima, start)
        peaks = [jnp.max(a, axis=0, keepdims=True) for a in acc]

        def totals(f, acc):
            for r in range(ROWS // 8):
                acc = [a + jnp.exp(values(f, r, t) - p) for a, p, t in zip(acc, peaks, group)]
            return acc

        start = [jnp.zeros((8, LANES), jnp.float32) for _ in group]
        acc = lax.fori_loop(0, blocks, totals, start)
        for a, p, t in zip(acc, peaks, group):
            out_ref[0:1, lanes(where[0, t])] = p
            out_ref[1:2, lanes(where[0, t])] = jnp.sum(a, axis=0, keepdims=True)


def exponentials_kernel(shapes, where, *refs):
    logits, (c_ref, out_ref, peak_ref, _) = refs[:len(shapes)], refs[len(shapes):]
    tiles = tile_list(shapes[:1])
    for k, ref in enumerate(logits):
        acc = None
        for t, (_, g, n) in enumerate(tiles):
            x = ref[0, g, :, n:n + LANES] + c_ref[:, lanes(where[0, t])]
            acc = x if acc is None else jnp.maximum(acc, x)
        peak_ref[...] = jnp.broadcast_to(jnp.max(acc, axis=1, keepdims=True), peak_ref.shape)
        top = peak_ref[...]
        for t, (_, g, n) in enumerate(tiles):
            x = ref[0, g, :, n:n + LANES] + c_ref[:, lanes(where[0, t])]
            out_ref[k, g, :, n:n + LANES] = jnp.exp(x - top).astype(jnp.bfloat16)


def scaled_rows(tiles, kernels, where, v_ref, row_ref):
    for d, k_ref in enumerate(kernels):
        for z in range(k_ref.shape[0]):
            acc = None
            for t, (_, g, n) in enumerate(tiles):
                x = k_ref[z, g, :, n:n + LANES].astype(jnp.float32) * v_ref[:, lanes(where[0, t])]
                acc = x if acc is None else acc + x
            first = (d * k_ref.shape[0] + z) * ROWS
            row_ref[first:first + ROWS, :] = acc
    return jnp.sum(row_ref[...], axis=1, keepdims=True)


def balance_kernel(shapes, where, *refs):
    kernels, (v_ref, out_ref, row_ref) = refs[:len(shapes)], refs[len(shapes):]
    tiles = tile_list(((1,) + shapes[0][1:],))
    total = scaled_rows(tiles, kernels, where, v_ref, row_ref)
    row_ref[...] = jnp.broadcast_to(1.0 / total, row_ref.shape)
    for t, (_, g, n) in enumerate(tiles):
        acc = jnp.zeros((ROWS, LANES), jnp.float32)
        for d, k_ref in enumerate(kernels):
            for z in range(k_ref.shape[0]):
                first = (d * k_ref.shape[0] + z) * ROWS
                acc = acc + k_ref[z, g, :, n:n + LANES].astype(jnp.float32) * row_ref[first:first + ROWS, :]
        out_ref[0:1, lanes(where[0, t])] = jnp.sum(acc, axis=0, keepdims=True)


def targets_kernel(shapes, widths, where, *refs):
    n = len(shapes)
    kernels, v_ref, x_refs, (out_ref, row_ref, w_ref) = refs[:n], refs[n], refs[n + 1:-3], refs[-3:]

    @pl.when(pl.program_id(0) == 0)
    def _():
        tiles = tile_list(((1,) + shapes[0][1:],))
        total = scaled_rows(tiles, kernels, where, v_ref, row_ref)
        row_ref[...] = jnp.broadcast_to(1.0 / total, row_ref.shape)
        for d, k_ref in enumerate(kernels):
            for z in range(k_ref.shape[0]):
                first = (d * k_ref.shape[0] + z) * ROWS
                scale = row_ref[first:first + ROWS, :]
                rows = pl.ds(pl.multiple_of(where[2, d * k_ref.shape[0] + z] * ROWS, ROWS), ROWS)
                for t, (_, g, n) in enumerate(tiles):
                    x = k_ref[z, g, :, n:n + LANES].astype(jnp.float32) * v_ref[:, lanes(where[0, t])]
                    w_ref[rows, lanes(where[1, t])] = (x * scale).astype(jnp.bfloat16)

    most = jnp.concatenate([x[...] for x in x_refs[:-1]], axis=0)
    first = sum(widths[:-1])
    acc = jnp.dot(w_ref[:, :first], most, preferred_element_type=jnp.float32)
    acc += jnp.dot(w_ref[:, first:], x_refs[-1][...], preferred_element_type=jnp.float32)
    out_ref[...] = acc.astype(out_ref.dtype)


def targets_call(where, kernels, v, datas):
    shapes = tuple(a.shape for a in kernels)
    rows = sum(s[0] for s in shapes) * ROWS
    widths = tuple(d.shape[0] for d in datas)
    depth, block = datas[0].shape[1], 1024
    vmem = pl.BlockSpec(memory_space=pltpu.VMEM)
    return pl.pallas_call(
        functools.partial(targets_kernel, shapes, widths),
        out_shape=jax.ShapeDtypeStruct((rows, depth), jnp.bfloat16),
        grid=(depth // block,),
        in_specs=[pl.BlockSpec(memory_space=pltpu.SMEM)] + [vmem] * (len(kernels) + 1)
        + [pl.BlockSpec((w, block), lambda n: (0, n)) for w in widths],
        out_specs=pl.BlockSpec((rows, block), lambda n: (0, n)),
        scratch_shapes=[
            pltpu.VMEM((rows, LANES), jnp.float32),
            pltpu.VMEM((rows, sum(widths)), jnp.bfloat16),
        ],
        compiler_params=pltpu.CompilerParams(vmem_limit_bytes=48 * 2**20),
    )(where, *kernels, v, *datas)


def balance_call(kernel, out_shape, where, kernels, v):
    shapes = tuple(a.shape for a in kernels)
    rows = sum(s[0] for s in shapes) * ROWS
    vmem = pl.BlockSpec(memory_space=pltpu.VMEM)
    return pl.pallas_call(
        functools.partial(kernel, shapes),
        out_shape=out_shape,
        in_specs=[pl.BlockSpec(memory_space=pltpu.SMEM)] + [vmem] * (len(kernels) + 1),
        out_specs=vmem,
        scratch_shapes=[pltpu.VMEM((rows, LANES), jnp.float32)],
        compiler_params=pltpu.CompilerParams(vmem_limit_bytes=32 * 2**20),
    )(where, *kernels, v)


def row_call(kernel, out_shape, where, logits, c):
    shapes = tuple(a.shape for a in logits)
    rows = shapes[0][0] * ROWS
    vmem = pl.BlockSpec(memory_space=pltpu.VMEM)
    return pl.pallas_call(
        functools.partial(kernel, shapes),
        out_shape=out_shape,
        in_specs=[pl.BlockSpec(memory_space=pltpu.SMEM)] + [vmem] * (len(logits) + 1),
        out_specs=vmem,
        scratch_shapes=[pltpu.VMEM((rows, LANES), jnp.float32)] * 2,
        compiler_params=pltpu.CompilerParams(vmem_limit_bytes=32 * 2**20),
    )(where, *logits, c)


SAMP_RINGS = (("core", 2), ("y", 4), ("zh", 2))
ALL_RINGS = (("core", 2), ("y", 4), (("zh", "zl"), 4), ("x", 4))


def around(x, axis, n):
    def shift(k):
        return lax.ppermute(x, axis, [(i, (i + k) % n) for i in range(n)])

    if n == 2:
        return [(x, shift(1))]
    left, right, across = shift(1), shift(-1), shift(2)
    return [(x, across), (left, right)]


def combine(pairs):
    peak = functools.reduce(jnp.maximum, [p[0] for pair in pairs for p in pair])
    totals = [sum(p[1] * jnp.exp(p[0] - peak) for p in pair) for pair in pairs]
    return jnp.stack([peak, sum(totals)])


def column_sum(x, rings):
    for axis, n in rings:
        x = sum(a + b for a, b in around(x, axis, n))
    return x


def column_sum_in_pairs(x):
    steps = (("core", 2, 1), ("y", 4, 1), ("y", 4, 2), ("zh", 2, 1), ("x", 4, 1), ("x", 4, 2))
    for axis, n, step in steps:
        x = x + lax.ppermute(x, axis, [(i, i ^ step) for i in range(n)])
    return x


def column_update(stats, rings):
    for axis, n in rings:
        stats = combine(around(stats, axis, n))
    return -(stats[0] + jnp.log(stats[1]))[None, :]


def lane_sums(x):
    acc = None
    for n in range(0, x.shape[1], LANES):
        v = x[:, n:n + LANES].astype(jnp.float32)
        acc = v * v if acc is None else acc + v * v
    return acc


def partial_kernel(noise_parts, jobs, known, scale, *refs):
    n_count = sum(noise_parts)
    x_count = 1 + max(x for _, xs in jobs for x in xs)
    where, old_n, old_x = refs[:3]
    n_refs, x_refs = refs[3:3 + n_count], refs[3 + n_count:3 + n_count + x_count]
    outs, (n_sq, x_row, acc, x_sq) = refs[3 + n_count + x_count:-4], refs[-4:]
    step = pl.program_id(0)
    parts, share, _ = acc.shape
    rows = parts * share
    starts = [sum(noise_parts[:q]) for q in range(len(noise_parts))]

    @pl.when(step == 0)
    def _():
        acc[...] = jnp.zeros_like(acc)
        n_sq[...] = jnp.zeros_like(n_sq)
        x_sq[...] = jnp.zeros_like(x_sq)

    places, first = [], 0
    for qs, xs in jobs:
        widths = [x_refs[x].shape[0] for x in xs]
        block = jnp.concatenate(
            [n_refs[starts[q] + p][...] for q in qs for p in range(noise_parts[q])], axis=0
        )
        others = jnp.concatenate([x_refs[x][...] for x in xs], axis=0)
        inner = lax.dot_general(
            block, others, (((1,), (1,)), ((), ())), preferred_element_type=jnp.float32
        )
        for i, q in enumerate(qs):
            at = first + i * sum(widths)
            part = inner[i * rows:(i + 1) * rows].reshape(parts, share, sum(widths))
            acc[:, :, at:at + sum(widths)] += part
            for x, width in zip(xs, widths):
                places.append((q, x, at))
                at += width
        first += len(qs) * sum(widths)
    x_starts = [sum(r.shape[0] for r in x_refs[:x]) for x in range(x_count)]
    for squares, blocks, seen in ((n_sq, n_refs, known[0]), (x_sq, x_refs, known[1])):
        start = 0
        for r in blocks:
            if start >= seen:
                squares[start:start + r.shape[0], :] += lane_sums(r[...])
            start += r.shape[0]

    @pl.when(step == pl.num_programs(0) - 1)
    def _():
        x_row[...] = lax.dot_general(
            jnp.ones((8, LANES), jnp.float32), x_sq[...], (((1,), (1,)), ((), ())),
            precision=lax.Precision.HIGHEST, preferred_element_type=jnp.float32,
        )[0:1]
        n_sq[...] = jnp.broadcast_to(jnp.sum(n_sq[...], axis=1, keepdims=True), n_sq.shape)
        if known[0]:
            n_sq[0:known[0], :] = old_n[...]
        if known[1]:
            x_row[:, 0:known[1]] = old_x[...]
        for d, out in zip((0, 1, -1, 2), outs):
            for z in range(2):
                f = (where[1] + z) % 2 * 4 + (where[0] + d + 4) % 4
                for q, x, at in places:
                    width = x_refs[x].shape[0]
                    own = n_sq[pl.ds(q * rows + f * share, share), 0:1]
                    other = x_row[:, x_starts[x]:x_starts[x] + width]
                    inner = acc[f, :, at:at + width]
                    out[z, :, at:at + width] = (own + other - 2.0 * inner) * scale


def partial_call(scale, parts, where, noises, datas, jobs, old_n=None, old_x=None):
    known = (0 if old_n is None else old_n.shape[0], 0 if old_x is None else old_x.shape[1])
    old_n = jnp.zeros((8, LANES), jnp.float32) if old_n is None else old_n
    old_x = jnp.zeros((1, LANES), jnp.float32) if old_x is None else old_x
    noise_parts = tuple(len(n) for n in noises)
    flat = [a for n in noises for a in n]
    rows, depth = sum(a.shape[0] for a in noises[0]), flat[0].shape[1]
    total = sum(len(qs) * sum(datas[x].shape[0] for x in xs) for qs, xs in jobs)
    share = rows // parts
    block = DEPTH
    out = (2, share, total)
    n_rows, columns = sum(a.shape[0] for a in flat), sum(d.shape[0] for d in datas)
    squares = [(n_rows, LANES), (1, columns)]
    *pieces, n_sq, x_row = pl.pallas_call(
        functools.partial(partial_kernel, noise_parts, jobs, known, scale),
        cost_estimate=pl.CostEstimate(flops=1, bytes_accessed=1, transcendentals=0),
        out_shape=[jax.ShapeDtypeStruct(o, jnp.float32) for o in [out] * 4 + squares],
        grid=(depth // block,),
        in_specs=[pl.BlockSpec(memory_space=pltpu.SMEM)]
        + [pl.BlockSpec(o.shape, lambda k: (0, 0)) for o in (old_n, old_x)]
        + [pl.BlockSpec((a.shape[0], block), lambda k: (0, k)) for a in (*flat, *datas)],
        out_specs=[pl.BlockSpec(out, lambda k: (0, 0, 0))] * 4
        + [pl.BlockSpec(o, lambda k: (0, 0)) for o in squares],
        scratch_shapes=[
            pltpu.VMEM((parts, share, total), jnp.float32),
            pltpu.VMEM((columns, LANES), jnp.float32),
        ],
        compiler_params=pltpu.CompilerParams(vmem_limit_bytes=48 * 2**20),
    )(where, old_n, old_x, *flat, *datas)
    return pieces, n_sq, x_row


def halves_kernel(u_ref, w_ref, a_ref, b_ref):
    a_ref[...] = u_ref[...]
    b_ref[...] = w_ref[...]


def halves_call(u, w):
    half, block = u.shape[0] // 2, 2048
    out = jax.ShapeDtypeStruct((half, u.shape[1]), u.dtype)
    return pl.pallas_call(
        halves_kernel,
        cost_estimate=pl.CostEstimate(flops=1, bytes_accessed=1, transcendentals=0),
        out_shape=[out, out],
        grid=(u.shape[1] // block,),
        in_specs=[pl.BlockSpec((half, block), lambda n: (0, n)), pl.BlockSpec((half, block), lambda n: (1, n))],
        out_specs=[pl.BlockSpec((half, block), lambda n: (0, n))] * 2,
    )(u, w)


def ring(x, shift):
    return lax.ppermute(x, "y", [(i, (i + shift) % 4) for i in range(4)])


def swap(x, axis):
    return lax.ppermute(x, axis, [(0, 1), (1, 0)])


SOURCES = [(0, 0, 0), (0, 0, 1), (0, 1, 0), (0, 1, 1), (-1, 0, 0), (-1, 0, 1), (1, 0, 0), (1, 0, 1)]
SOURCES += [(-1, 1, 0), (-1, 1, 1), (1, 1, 0), (1, 1, 1), (-2, 0, 0), (2, 0, 1), (-2, 1, 0), (2, 1, 1)]
ALONG_X = (0, 1, -1, 2)


def along_x(x, step):
    return lax.ppermute(x, "x", [(i, (i + step) % 4) for i in range(4)])


def tables(parts):
    zh, y, core = (lax.axis_index(a) for a in ("zh", "y", "core"))
    where, place = [], []
    for dz in range(2):
        for s, (dy, dc, half) in enumerate(SOURCES):
            inside = ((y + dy + 4) % 4 * 2 + (core + dc) % 2) * 2 + half
            where.append((zh + dz) % 2 * 16 + inside)
            place.append(16 + inside if dz else jnp.int32(s))
    x, zl = lax.axis_index("x"), lax.axis_index("zl")
    rows = [(zl + z) % 2 * 4 + (x + d + 4) % 4 for d in ALONG_X for z in range(2)]
    rows = jnp.pad(jnp.stack(rows), (0, len(where) - len(rows)))
    return jnp.stack([jnp.stack(where), jnp.stack(place), rows]).astype(jnp.int32)


def local(noise, data):
    temper = 0.5 / math.sqrt(F)
    scale = -1.0 / (F * temper)
    parts = 8
    half = noise.shape[0] // 2
    call = functools.partial(partial_call, scale, parts)
    where = tables(parts)
    here = jnp.stack([lax.axis_index("x"), lax.axis_index("zl")]).astype(jnp.int32)
    hold = lax.optimization_barrier

    u, w = ring(data, 1), ring(data, -1)
    far = swap(noise, "zh")
    data_c = swap(data, "core")
    (k0, k1, k3, k2), n_sq, x_row = call(here, [(noise,)], [data, data_c], (((0,), (0, 1)),))
    k1, k3 = along_x(k1, 1), along_x(k3, -1)
    k1, k2, k3 = hold((k1, k2, k3))
    k2 = along_x(k2, 2)
    u, w, data_c, data, k0, k1, k2, k3 = hold((u, w, data_c, data, k0, k1, k2, k3))

    ua, wb = halves_call(u, w)
    ua, wb, u, w, data = hold((ua, wb, u, w, data))
    u3, w3 = ring(ua, 1), ring(wb, -1)
    u_c, w_c = swap(u, "core"), swap(w, "core")
    other = swap(data, "zh")
    noises = [(noise,), (far,)]
    jobs = (((0, 1), (2, 3)), ((1,), (0, 1)))
    (a0, a1, a3, a2), n_sq, _ = call(here, noises, [data, data_c, u, w], jobs, n_sq, x_row)
    u_c, w_c, a0, a1, a2, a3 = hold((u_c, w_c, a0, a1, a2, a3))
    a1, a3 = along_x(a1, 1), along_x(a3, -1)
    (b0, b1, b3, b2), _, _ = call(here, noises, [u_c, w_c], (((0, 1), (0, 1)),), n_sq)
    a2 = along_x(a2, 2)
    b1, b3 = along_x(b1, 1), along_x(b3, -1)
    u3, w3, a1, a3, b0, b2 = hold((u3, w3, a1, a3, b0, b2))

    u3_c, w3_c = swap(u3, "core"), swap(w3, "core")
    (c0, c1, c3, c2), _, _ = call(here, noises, [u3, w3, u3_c, w3_c], (((0, 1), (0, 1, 2, 3)),), n_sq)
    b2 = along_x(b2, 2)
    c1, c3, c2 = along_x(c1, 1), along_x(c3, -1), along_x(c2, 2)
    k, a = k0 + k1 + k2 + k3, a0 + a1 + a2 + a3

    def early(z):
        return jnp.stack([
            jnp.concatenate([k[z], a[z][:, :512]], axis=1),
            jnp.concatenate([a[z][:, 1024:], a[z][:, 512:1024]], axis=1),
        ])

    b2, c1, c2, c3, other = hold((b2, c1, c2, c3, other))
    b, c = b0 + b1 + b2 + b3, c0 + c1 + c2 + c3

    def late(z):
        return jnp.stack([
            jnp.concatenate([p[z][:, i * 512:(i + 1) * 512] for p in (b, c)], axis=1) for i in range(2)
        ])

    def across_z(x, step):
        return lax.ppermute(x, ("zh", "zl"), [(i, i ^ step) for i in range(4)])

    mine, theirs = (jnp.concatenate([early(z), late(z)], axis=2) for z in range(2))
    mine, theirs, other = hold((mine, theirs, other))
    others = lax.all_gather(other, ("y", "core"), axis=0, tiled=True)
    out = jax.ShapeDtypeStruct((2, SAMPLES), jnp.float32)

    once = lax.axis_index("x") // 8 + 1

    once = lax.axis_index("x") // 8 + 1

    def to_owners(_, acc):
        return acc + jnp.stack([
            mine[0] + across_z(theirs[0], 1), across_z(mine[1], 2) + across_z(theirs[1], 3)
        ])

    def spread(_, c):
        return column_update(row_call(sinkhorn_kernel, out, where, [own[None]], c), ALL_RINGS)

    own = lax.fori_loop(0, once, to_owners, jnp.zeros(mine.shape, jnp.float32))
    pair = lax.ppermute(own, "zl", [(0, 1), (1, 0)])
    c = lax.fori_loop(0, once, spread, jnp.zeros((1, SAMPLES), jnp.float32))
    c, pair = hold((c, pair))
    shape = jax.ShapeDtypeStruct((2,) + own.shape, jnp.bfloat16)
    both = row_call(exponentials_kernel, shape, where, [own[None], pair[None]], c)
    kernels = [both] + [along_x(both, -d) for d in ALONG_X[1:]]

    sums = jax.ShapeDtypeStruct((1, SAMPLES), jnp.float32)

    def balance(_, v):
        return 1.0 / column_sum_in_pairs(balance_call(balance_kernel, sums, where, [both], v))

    v = lax.fori_loop(0, once, balance, jnp.ones((1, SAMPLES), jnp.float32))
    blocks = [data, data_c, u, w, u_c, w_c, u3, w3, u3_c, w3_c]
    for _ in range(2, ITERS):
        v = 1.0 / column_sum(balance_call(balance_kernel, sums, where, kernels, v), SAMP_RINGS)
    c = c + jnp.log(v)
    share = SAMPLES // parts
    start = (lax.axis_index("zl") * 4 + lax.axis_index("x")) * share
    column_out = lax.dynamic_slice_in_dim(c[0] * temper, start, share, 0)
    return (targets_call(where, kernels, v, [*blocks, others]), column_out)


def solution(mesh):
    fine = Mesh(mesh.devices.reshape(2, 4, 2, 2, 4), ("zh", "y", "core", "zl", "x"))
    samp, feat = ("zh", "y", "core"), FEAT
    in_specs = (P(samp, feat), P(samp, feat))
    out_specs = (P(samp, feat), P(feat))
    return jax.shard_map(local, mesh=fine, in_specs=in_specs, out_specs=out_specs, check_vma=False)
```

```python
import functools
import math

import jax
import jax.numpy as jnp
from jax import lax
from jax.experimental import pallas as pl
from jax.experimental.pallas import tpu as pltpu
from jax.sharding import Mesh, PartitionSpec as P

F = 32768
ITERS = 3
SAMPLES = 4096
LANES = 128
ROWS = 32
GROUP = 4
DEPTH = 2048
FEAT = ("zl", "x")


def tile_list(shapes):
    return [
        (k, g, n)
        for k, (_, groups, _, width) in enumerate(shapes)
        for g in range(groups)
        for n in range(0, width, LANES)
    ]


def row_pass(tiles, blocks, logits, where, c_ref, peak_ref, row_ref):
    def tile(f, t):
        k, g, n = tiles[t]
        return logits[k][f, g, :, n:n + LANES] + c_ref[:, lanes(where[0, t])]

    def maxima(f, _):
        acc = tile(f, 0)
        for t in range(1, len(tiles)):
            acc = jnp.maximum(acc, tile(f, t))
        peak_ref[pl.ds(f * ROWS, ROWS), :] = acc
        return 0

    lax.fori_loop(0, blocks, maxima, 0)
    peak = jnp.max(peak_ref[...], axis=1, keepdims=True)
    peak_ref[...] = jnp.broadcast_to(peak, peak_ref.shape)

    def totals(f, _):
        top = peak_ref[pl.ds(f * ROWS, ROWS), :]
        acc = jnp.exp(tile(f, 0) - top)
        for t in range(1, len(tiles)):
            acc = acc + jnp.exp(tile(f, t) - top)
        row_ref[pl.ds(f * ROWS, ROWS), :] = acc
        return 0

    lax.fori_loop(0, blocks, totals, 0)
    return jnp.sum(row_ref[...], axis=1, keepdims=True)


def lanes(tile):
    return pl.ds(pl.multiple_of(tile * LANES, LANES), LANES)


def sinkhorn_kernel(shapes, where, *refs):
    logits, (c_ref, out_ref, peak_ref, row_ref) = refs[:len(shapes)], refs[len(shapes):]
    tiles = tile_list(shapes)
    blocks = shapes[0][0]
    total = row_pass(tiles, blocks, logits, where, c_ref, peak_ref, row_ref)
    row_ref[...] = jnp.broadcast_to(-(peak_ref[:, 0:1] + jnp.log(total)), row_ref.shape)
    for first in range(0, len(tiles), GROUP):
        group = range(first, first + GROUP)

        def values(f, r, t):
            k, g, n = tiles[t]
            rows = row_ref[pl.ds(f * ROWS + r * 8, 8), :]
            return logits[k][f, g, r * 8:(r + 1) * 8, n:n + LANES] + rows

        def maxima(f, acc):
            for r in range(ROWS // 8):
                acc = [jnp.maximum(a, values(f, r, t)) for a, t in zip(acc, group)]
            return acc

        start = [jnp.full((8, LANES), -jnp.inf, jnp.float32) for _ in group]
        acc = lax.fori_loop(0, blocks, maxima, start)
        peaks = [jnp.max(a, axis=0, keepdims=True) for a in acc]

        def totals(f, acc):
            for r in range(ROWS // 8):
                acc = [a + jnp.exp(values(f, r, t) - p) for a, p, t in zip(acc, peaks, group)]
            return acc

        start = [jnp.zeros((8, LANES), jnp.float32) for _ in group]
        acc = lax.fori_loop(0, blocks, totals, start)
        for a, p, t in zip(acc, peaks, group):
            out_ref[0:1, lanes(where[0, t])] = p
            out_ref[1:2, lanes(where[0, t])] = jnp.sum(a, axis=0, keepdims=True)


def exponentials_kernel(shapes, where, *refs):
    logits, (c_ref, out_ref, peak_ref, _) = refs[:len(shapes)], refs[len(shapes):]
    tiles = tile_list(shapes[:1])
    for k, ref in enumerate(logits):
        acc = None
        for t, (_, g, n) in enumerate(tiles):
            x = ref[0, g, :, n:n + LANES] + c_ref[:, lanes(where[0, t])]
            acc = x if acc is None else jnp.maximum(acc, x)
        peak_ref[...] = jnp.broadcast_to(jnp.max(acc, axis=1, keepdims=True), peak_ref.shape)
        top = peak_ref[...]
        for t, (_, g, n) in enumerate(tiles):
            x = ref[0, g, :, n:n + LANES] + c_ref[:, lanes(where[0, t])]
            out_ref[k, g, :, n:n + LANES] = jnp.exp(x - top).astype(jnp.bfloat16)


def scaled_rows(tiles, kernels, where, v_ref, row_ref):
    for d, k_ref in enumerate(kernels):
        for z in range(k_ref.shape[0]):
            acc = None
            for t, (_, g, n) in enumerate(tiles):
                x = k_ref[z, g, :, n:n + LANES].astype(jnp.float32) * v_ref[:, lanes(where[0, t])]
                acc = x if acc is None else acc + x
            first = (d * k_ref.shape[0] + z) * ROWS
            row_ref[first:first + ROWS, :] = acc
    return jnp.sum(row_ref[...], axis=1, keepdims=True)


def balance_kernel(shapes, where, *refs):
    kernels, (v_ref, out_ref, row_ref) = refs[:len(shapes)], refs[len(shapes):]
    tiles = tile_list(((1,) + shapes[0][1:],))
    total = scaled_rows(tiles, kernels, where, v_ref, row_ref)
    row_ref[...] = jnp.broadcast_to(1.0 / total, row_ref.shape)
    for t, (_, g, n) in enumerate(tiles):
        acc = jnp.zeros((ROWS, LANES), jnp.float32)
        for d, k_ref in enumerate(kernels):
            for z in range(k_ref.shape[0]):
                first = (d * k_ref.shape[0] + z) * ROWS
                acc = acc + k_ref[z, g, :, n:n + LANES].astype(jnp.float32) * row_ref[first:first + ROWS, :]
        out_ref[0:1, lanes(where[0, t])] = jnp.sum(acc, axis=0, keepdims=True)


def targets_kernel(shapes, widths, where, *refs):
    n = len(shapes)
    kernels, v_ref, x_refs, (out_ref, row_ref, w_ref) = refs[:n], refs[n], refs[n + 1:-3], refs[-3:]

    @pl.when(pl.program_id(0) == 0)
    def _():
        tiles = tile_list(((1,) + shapes[0][1:],))
        total = scaled_rows(tiles, kernels, where, v_ref, row_ref)
        row_ref[...] = jnp.broadcast_to(1.0 / total, row_ref.shape)
        for d, k_ref in enumerate(kernels):
            for z in range(k_ref.shape[0]):
                first = (d * k_ref.shape[0] + z) * ROWS
                scale = row_ref[first:first + ROWS, :]
                rows = pl.ds(pl.multiple_of(where[2, d * k_ref.shape[0] + z] * ROWS, ROWS), ROWS)
                for t, (_, g, n) in enumerate(tiles):
                    x = k_ref[z, g, :, n:n + LANES].astype(jnp.float32) * v_ref[:, lanes(where[0, t])]
                    w_ref[rows, lanes(where[1, t])] = (x * scale).astype(jnp.bfloat16)

    everything = jnp.concatenate([x[...] for x in x_refs], axis=0)
    acc = jnp.dot(w_ref[...], everything, preferred_element_type=jnp.float32)
    out_ref[...] = acc.astype(out_ref.dtype)


def targets_call(where, kernels, v, datas):
    shapes = tuple(a.shape for a in kernels)
    rows = sum(s[0] for s in shapes) * ROWS
    widths = tuple(d.shape[0] for d in datas)
    depth, block = datas[0].shape[1], 1024
    vmem = pl.BlockSpec(memory_space=pltpu.VMEM)
    return pl.pallas_call(
        functools.partial(targets_kernel, shapes, widths),
        out_shape=jax.ShapeDtypeStruct((rows, depth), jnp.bfloat16),
        grid=(depth // block,),
        in_specs=[pl.BlockSpec(memory_space=pltpu.SMEM)] + [vmem] * (len(kernels) + 1)
        + [pl.BlockSpec((w, block), lambda n: (0, n)) for w in widths],
        out_specs=pl.BlockSpec((rows, block), lambda n: (0, n)),
        scratch_shapes=[
            pltpu.VMEM((rows, LANES), jnp.float32),
            pltpu.VMEM((rows, sum(widths)), jnp.bfloat16),
        ],
        compiler_params=pltpu.CompilerParams(vmem_limit_bytes=48 * 2**20),
    )(where, *kernels, v, *datas)


def balance_call(kernel, out_shape, where, kernels, v):
    shapes = tuple(a.shape for a in kernels)
    rows = sum(s[0] for s in shapes) * ROWS
    vmem = pl.BlockSpec(memory_space=pltpu.VMEM)
    return pl.pallas_call(
        functools.partial(kernel, shapes),
        out_shape=out_shape,
        in_specs=[pl.BlockSpec(memory_space=pltpu.SMEM)] + [vmem] * (len(kernels) + 1),
        out_specs=vmem,
        scratch_shapes=[pltpu.VMEM((rows, LANES), jnp.float32)],
        compiler_params=pltpu.CompilerParams(vmem_limit_bytes=32 * 2**20),
    )(where, *kernels, v)


def row_call(kernel, out_shape, where, logits, c):
    shapes = tuple(a.shape for a in logits)
    rows = shapes[0][0] * ROWS
    vmem = pl.BlockSpec(memory_space=pltpu.VMEM)
    return pl.pallas_call(
        functools.partial(kernel, shapes),
        out_shape=out_shape,
        in_specs=[pl.BlockSpec(memory_space=pltpu.SMEM)] + [vmem] * (len(logits) + 1),
        out_specs=vmem,
        scratch_shapes=[pltpu.VMEM((rows, LANES), jnp.float32)] * 2,
        compiler_params=pltpu.CompilerParams(vmem_limit_bytes=32 * 2**20),
    )(where, *logits, c)


SAMP_RINGS = (("core", 2), ("y", 4), ("zh", 2))
ALL_RINGS = (("core", 2), ("y", 4), (("zh", "zl"), 4), ("x", 4))


def around(x, axis, n):
    def shift(k):
        return lax.ppermute(x, axis, [(i, (i + k) % n) for i in range(n)])

    if n == 2:
        return [(x, shift(1))]
    left, right, across = shift(1), shift(-1), shift(2)
    return [(x, across), (left, right)]


def combine(pairs):
    peak = functools.reduce(jnp.maximum, [p[0] for pair in pairs for p in pair])
    totals = [sum(p[1] * jnp.exp(p[0] - peak) for p in pair) for pair in pairs]
    return jnp.stack([peak, sum(totals)])


def column_sum(x, rings):
    for axis, n in rings:
        x = sum(a + b for a, b in around(x, axis, n))
    return x


def column_sum_in_pairs(x):
    steps = (("core", 2, 1), ("y", 4, 1), ("y", 4, 2), ("zh", 2, 1), ("x", 4, 1), ("x", 4, 2))
    for axis, n, step in steps:
        x = x + lax.ppermute(x, axis, [(i, i ^ step) for i in range(n)])
    return x


def column_update(stats, rings):
    for axis, n in rings:
        stats = combine(around(stats, axis, n))
    return -(stats[0] + jnp.log(stats[1]))[None, :]


def lane_sums(x):
    acc = None
    for n in range(0, x.shape[1], LANES):
        v = x[:, n:n + LANES].astype(jnp.float32)
        acc = v * v if acc is None else acc + v * v
    return acc


def partial_kernel(noise_parts, jobs, known, scale, *refs):
    n_count = sum(noise_parts)
    x_count = 1 + max(x for _, xs in jobs for x in xs)
    where, old_n, old_x = refs[:3]
    n_refs, x_refs = refs[3:3 + n_count], refs[3 + n_count:3 + n_count + x_count]
    outs, (n_sq, x_row, acc, x_sq) = refs[3 + n_count + x_count:-4], refs[-4:]
    step = pl.program_id(0)
    parts, share, _ = acc.shape
    rows = parts * share
    starts = [sum(noise_parts[:q]) for q in range(len(noise_parts))]

    @pl.when(step == 0)
    def _():
        acc[...] = jnp.zeros_like(acc)
        n_sq[...] = jnp.zeros_like(n_sq)
        x_sq[...] = jnp.zeros_like(x_sq)

    places, first = [], 0
    for qs, xs in jobs:
        widths = [x_refs[x].shape[0] for x in xs]
        block = jnp.concatenate(
            [n_refs[starts[q] + p][...] for q in qs for p in range(noise_parts[q])], axis=0
        )
        others = jnp.concatenate([x_refs[x][...] for x in xs], axis=0)
        inner = lax.dot_general(
            block, others, (((1,), (1,)), ((), ())), preferred_element_type=jnp.float32
        )
        for i, q in enumerate(qs):
            at = first + i * sum(widths)
            part = inner[i * rows:(i + 1) * rows].reshape(parts, share, sum(widths))
            acc[:, :, at:at + sum(widths)] += part
            for x, width in zip(xs, widths):
                places.append((q, x, at))
                at += width
        first += len(qs) * sum(widths)
    x_starts = [sum(r.shape[0] for r in x_refs[:x]) for x in range(x_count)]
    for squares, blocks, seen in ((n_sq, n_refs, known[0]), (x_sq, x_refs, known[1])):
        start = 0
        for r in blocks:
            if start >= seen:
                squares[start:start + r.shape[0], :] += lane_sums(r[...])
            start += r.shape[0]

    @pl.when(step == pl.num_programs(0) - 1)
    def _():
        x_row[...] = lax.dot_general(
            jnp.ones((8, LANES), jnp.float32), x_sq[...], (((1,), (1,)), ((), ())),
            precision=lax.Precision.HIGHEST, preferred_element_type=jnp.float32,
        )[0:1]
        n_sq[...] = jnp.broadcast_to(jnp.sum(n_sq[...], axis=1, keepdims=True), n_sq.shape)
        if known[0]:
            n_sq[0:known[0], :] = old_n[...]
        if known[1]:
            x_row[:, 0:known[1]] = old_x[...]
        for d, out in zip((0, 1, -1, 2), outs):
            for z in range(2):
                f = (where[1] + z) % 2 * 4 + (where[0] + d + 4) % 4
                for q, x, at in places:
                    width = x_refs[x].shape[0]
                    own = n_sq[pl.ds(q * rows + f * share, share), 0:1]
                    other = x_row[:, x_starts[x]:x_starts[x] + width]
                    inner = acc[f, :, at:at + width]
                    out[z, :, at:at + width] = (own + other - 2.0 * inner) * scale


def partial_call(scale, parts, where, noises, datas, jobs, old_n=None, old_x=None):
    known = (0 if old_n is None else old_n.shape[0], 0 if old_x is None else old_x.shape[1])
    old_n = jnp.zeros((8, LANES), jnp.float32) if old_n is None else old_n
    old_x = jnp.zeros((1, LANES), jnp.float32) if old_x is None else old_x
    noise_parts = tuple(len(n) for n in noises)
    flat = [a for n in noises for a in n]
    rows, depth = sum(a.shape[0] for a in noises[0]), flat[0].shape[1]
    total = sum(len(qs) * sum(datas[x].shape[0] for x in xs) for qs, xs in jobs)
    share = rows // parts
    block = DEPTH
    out = (2, share, total)
    n_rows, columns = sum(a.shape[0] for a in flat), sum(d.shape[0] for d in datas)
    squares = [(n_rows, LANES), (1, columns)]
    *pieces, n_sq, x_row = pl.pallas_call(
        functools.partial(partial_kernel, noise_parts, jobs, known, scale),
        cost_estimate=pl.CostEstimate(flops=1, bytes_accessed=1, transcendentals=0),
        out_shape=[jax.ShapeDtypeStruct(o, jnp.float32) for o in [out] * 4 + squares],
        grid=(depth // block,),
        in_specs=[pl.BlockSpec(memory_space=pltpu.SMEM)]
        + [pl.BlockSpec(o.shape, lambda k: (0, 0)) for o in (old_n, old_x)]
        + [pl.BlockSpec((a.shape[0], block), lambda k: (0, k)) for a in (*flat, *datas)],
        out_specs=[pl.BlockSpec(out, lambda k: (0, 0, 0))] * 4
        + [pl.BlockSpec(o, lambda k: (0, 0)) for o in squares],
        scratch_shapes=[
            pltpu.VMEM((parts, share, total), jnp.float32),
            pltpu.VMEM((columns, LANES), jnp.float32),
        ],
        compiler_params=pltpu.CompilerParams(vmem_limit_bytes=48 * 2**20),
    )(where, old_n, old_x, *flat, *datas)
    return pieces, n_sq, x_row


def halves_kernel(u_ref, w_ref, a_ref, b_ref):
    a_ref[...] = u_ref[...]
    b_ref[...] = w_ref[...]


def halves_call(u, w):
    half, block = u.shape[0] // 2, 2048
    out = jax.ShapeDtypeStruct((half, u.shape[1]), u.dtype)
    return pl.pallas_call(
        halves_kernel,
        cost_estimate=pl.CostEstimate(flops=1, bytes_accessed=1, transcendentals=0),
        out_shape=[out, out],
        grid=(u.shape[1] // block,),
        in_specs=[pl.BlockSpec((half, block), lambda n: (0, n)), pl.BlockSpec((half, block), lambda n: (1, n))],
        out_specs=[pl.BlockSpec((half, block), lambda n: (0, n))] * 2,
    )(u, w)


def ring(x, shift):
    return lax.ppermute(x, "y", [(i, (i + shift) % 4) for i in range(4)])


def swap(x, axis):
    return lax.ppermute(x, axis, [(0, 1), (1, 0)])


SOURCES = [(0, 0, 0), (0, 0, 1), (0, 1, 0), (0, 1, 1), (-1, 0, 0), (-1, 0, 1), (1, 0, 0), (1, 0, 1)]
SOURCES += [(-1, 1, 0), (-1, 1, 1), (1, 1, 0), (1, 1, 1), (-2, 0, 0), (2, 0, 1), (-2, 1, 0), (2, 1, 1)]
ALONG_X = (0, 1, -1, 2)


def along_x(x, step):
    return lax.ppermute(x, "x", [(i, (i + step) % 4) for i in range(4)])


def tables(parts):
    zh, y, core = (lax.axis_index(a) for a in ("zh", "y", "core"))
    where, place = [], []
    for dz in range(2):
        for s, (dy, dc, half) in enumerate(SOURCES):
            inside = ((y + dy + 4) % 4 * 2 + (core + dc) % 2) * 2 + half
            where.append((zh + dz) % 2 * 16 + inside)
            place.append(16 + inside if dz else jnp.int32(s))
    x, zl = lax.axis_index("x"), lax.axis_index("zl")
    rows = [(zl + z) % 2 * 4 + (x + d + 4) % 4 for d in ALONG_X for z in range(2)]
    rows = jnp.pad(jnp.stack(rows), (0, len(where) - len(rows)))
    return jnp.stack([jnp.stack(where), jnp.stack(place), rows]).astype(jnp.int32)


def local(noise, data):
    temper = 0.5 / math.sqrt(F)
    scale = -1.0 / (F * temper)
    parts = 8
    half = noise.shape[0] // 2
    call = functools.partial(partial_call, scale, parts)
    where = tables(parts)
    here = jnp.stack([lax.axis_index("x"), lax.axis_index("zl")]).astype(jnp.int32)
    hold = lax.optimization_barrier

    u, w = ring(data, 1), ring(data, -1)
    far = swap(noise, "zh")
    data_c = swap(data, "core")
    (k0, k1, k3, k2), n_sq, x_row = call(here, [(noise,)], [data, data_c], (((0,), (0, 1)),))
    k1, k3 = along_x(k1, 1), along_x(k3, -1)
    k1, k2, k3 = hold((k1, k2, k3))
    k2 = along_x(k2, 2)
    u, w, data_c, data, k0, k1, k2, k3 = hold((u, w, data_c, data, k0, k1, k2, k3))

    ua, wb = halves_call(u, w)
    ua, wb, u, w, data = hold((ua, wb, u, w, data))
    u3, w3 = ring(ua, 1), ring(wb, -1)
    u_c, w_c = swap(u, "core"), swap(w, "core")
    other = swap(data, "zh")
    noises = [(noise,), (far,)]
    jobs = (((0, 1), (2, 3)), ((1,), (0, 1)))
    (a0, a1, a3, a2), n_sq, _ = call(here, noises, [data, data_c, u, w], jobs, n_sq, x_row)
    u_c, w_c, a0, a1, a2, a3 = hold((u_c, w_c, a0, a1, a2, a3))
    a1, a3 = along_x(a1, 1), along_x(a3, -1)
    (b0, b1, b3, b2), _, _ = call(here, noises, [u_c, w_c], (((0, 1), (0, 1)),), n_sq)
    a2 = along_x(a2, 2)
    b1, b3 = along_x(b1, 1), along_x(b3, -1)
    u3, w3, a1, a3, b0, b2 = hold((u3, w3, a1, a3, b0, b2))

    u3_c, w3_c = swap(u3, "core"), swap(w3, "core")
    (c0, c1, c3, c2), _, _ = call(here, noises, [u3, w3, u3_c, w3_c], (((0, 1), (0, 1, 2, 3)),), n_sq)
    b2 = along_x(b2, 2)
    c1, c3, c2 = along_x(c1, 1), along_x(c3, -1), along_x(c2, 2)
    k, a = k0 + k1 + k2 + k3, a0 + a1 + a2 + a3

    def early(z):
        return jnp.stack([
            jnp.concatenate([k[z], a[z][:, :512]], axis=1),
            jnp.concatenate([a[z][:, 1024:], a[z][:, 512:1024]], axis=1),
        ])

    b2, c1, c2, c3, other = hold((b2, c1, c2, c3, other))
    b, c = b0 + b1 + b2 + b3, c0 + c1 + c2 + c3

    def late(z):
        return jnp.stack([
            jnp.concatenate([p[z][:, i * 512:(i + 1) * 512] for p in (b, c)], axis=1) for i in range(2)
        ])

    def across_z(x, step):
        return lax.ppermute(x, ("zh", "zl"), [(i, i ^ step) for i in range(4)])

    mine, theirs = (jnp.concatenate([early(z), late(z)], axis=2) for z in range(2))
    mine, theirs, other = hold((mine, theirs, other))
    others = lax.all_gather(other, ("y", "core"), axis=0, tiled=True)
    out = jax.ShapeDtypeStruct((2, SAMPLES), jnp.float32)

    once = lax.axis_index("x") // 8 + 1

    once = lax.axis_index("x") // 8 + 1

    def to_owners(_, acc):
        return acc + jnp.stack([
            mine[0] + across_z(theirs[0], 1), across_z(mine[1], 2) + across_z(theirs[1], 3)
        ])

    def spread(_, c):
        return column_update(row_call(sinkhorn_kernel, out, where, [own[None]], c), ALL_RINGS)

    own = lax.fori_loop(0, once, to_owners, jnp.zeros(mine.shape, jnp.float32))
    pair = lax.ppermute(own, "zl", [(0, 1), (1, 0)])
    c = lax.fori_loop(0, once, spread, jnp.zeros((1, SAMPLES), jnp.float32))
    c, pair = hold((c, pair))
    shape = jax.ShapeDtypeStruct((2,) + own.shape, jnp.bfloat16)
    both = row_call(exponentials_kernel, shape, where, [own[None], pair[None]], c)
    kernels = [both] + [along_x(both, -d) for d in ALONG_X[1:]]

    sums = jax.ShapeDtypeStruct((1, SAMPLES), jnp.float32)

    def balance(_, v):
        return 1.0 / column_sum_in_pairs(balance_call(balance_kernel, sums, where, [both], v))

    v = lax.fori_loop(0, once, balance, jnp.ones((1, SAMPLES), jnp.float32))
    blocks = [data, data_c, u, w, u_c, w_c, u3, w3, u3_c, w3_c]
    for _ in range(2, ITERS):
        v = 1.0 / column_sum(balance_call(balance_kernel, sums, where, kernels, v), SAMP_RINGS)
    c = c + jnp.log(v)
    share = SAMPLES // parts
    start = (lax.axis_index("zl") * 4 + lax.axis_index("x")) * share
    column_out = lax.dynamic_slice_in_dim(c[0] * temper, start, share, 0)
    return (targets_call(where, kernels, v, [*blocks, others]), column_out)


def solution(mesh):
    fine = Mesh(mesh.devices.reshape(2, 4, 2, 2, 4), ("zh", "y", "core", "zl", "x"))
    samp, feat = ("zh", "y", "core"), FEAT
    in_specs = (P(samp, feat), P(samp, feat))
    out_specs = (P(samp, feat), P(feat))
    return jax.shard_map(local, mesh=fine, in_specs=in_specs, out_specs=out_specs, check_vma=False)
```
